128 devices in a mesh: row: 16 (over x_hi, z, core), col: 8 (over x_lo, y).
Axes of the slice: x: 4 (x_hi: 2, x_lo: 2; x = x_hi * 2 + x_lo), y: 4, z: 4, core: 2. Of those that a mesh axis runs over, the one named last changes fastest.
Arguments:
- sign_iterate: float32 [6144, 6144], P('row', 'col'), may hold values from -1.25 to 1.25
- operand_pattern: int32 [1024, 1024], P('row', 'col'), may hold values from 0 to 1, as said below
- product_pattern: int32 [1024, 1024], P('row', 'col'), may hold values from 0 to 1, as said below
Outputs:
- sign_next: float32 [6144, 6144], P('row', 'col')
- defect: float32 [], replicated
The draws below stay inside these ranges and needn't reach their ends.
Inputs may be any that keep to these rules, and one draw needn't show every extreme that they name: `operand_pattern`: symmetric, 1 on the diagonal. `product_pattern`: symmetric, 1 on the diagonal and wherever operand_pattern is 1.
All inputs are finite; a program needn't handle non-finite values.
Results may differ from the reference program's by a relative error of at most 0.000076.
Values sent between devices are 32-bit elements; how exact they have to be, the bound alone decides.
No kernel may reach another device: no remote copies, remote signals or barrier semaphores. Data moves between devices by JAX's collectives and lax.ppermute only.
A program may use at most 128 MiB of HBM per device.

```python
import jax
import jax.numpy as jnp
from jax import lax

BS = 6
BR = 64
NB = 1024


cell_side = 64


operand_reach = 3600


product_reach = 8100


def squared_distances(key):
    key = jax.random.fold_in(key, 29)
    offset_key = jax.random.fold_in(key, 3)
    order_key = jax.random.fold_in(key, 7)
    blocks = NB // BR
    across = blocks // 2
    index = jnp.arange(NB, dtype=jnp.int32)
    placed = jax.random.permutation(order_key, index).astype(jnp.int32)
    block = placed // BR
    cell_x = block % across
    cell_y = block // across
    offsets = jax.random.randint(offset_key, (NB, 3), 0, cell_side, dtype=jnp.int32)
    pos_x = cell_x * cell_side + offsets[:, 0]
    pos_y = cell_y * cell_side + offsets[:, 1]
    pos_z = offsets[:, 2]
    period_x = across * cell_side
    period_y = 2 * cell_side
    diff_x = jnp.abs(pos_x[:, None] - pos_x[None, :])
    diff_x = jnp.minimum(diff_x, period_x - diff_x)
    diff_y = jnp.abs(pos_y[:, None] - pos_y[None, :])
    diff_y = jnp.minimum(diff_y, period_y - diff_y)
    diff_z = jnp.abs(pos_z[:, None] - pos_z[None, :])
    return diff_x * diff_x + diff_y * diff_y + diff_z * diff_z


def draw_operand_pattern(key, part):
    distances = squared_distances(key)
    return (distances <= operand_reach).astype(jnp.int32)


def draw_product_pattern(key, part):
    distances = squared_distances(key)
    return (distances <= product_reach).astype(jnp.int32)


def draw_sign_iterate(key, part):
    key = jax.random.fold_in(key, 11)
    noise_key, level_key, sign_key = jax.random.split(key, 3)
    order = BS * NB
    noise = jnp.clip(jax.random.normal(noise_key, (order, order), jnp.float32), -5.0, 5.0)
    molecule_index = jnp.arange(order) // BS
    same_molecule = molecule_index[:, None] == molecule_index[None, :]
    level = jax.random.uniform(level_key, (order,), jnp.float32, 0.2, 0.8)
    flips = jnp.where(jax.random.uniform(sign_key, (order,), jnp.float32) > 0.5, 1.0, -1.0)
    values = jnp.where(same_molecule, 0.08 * noise, 0.008 * noise)
    on_diagonal = jnp.arange(order)[:, None] == jnp.arange(order)[None, :]
    return values + jnp.where(on_diagonal, (level * flips)[:, None], 0.0)


def setup_inputs(seed: int = 0) -> dict:
    key_of = jax.random.split(jax.random.key(seed), 4)
    sign_iterate = draw_sign_iterate(jax.random.fold_in(key_of[3], 71), 0)
    operand_pattern = draw_operand_pattern(jax.random.fold_in(key_of[3], 71), 0)
    product_pattern = draw_product_pattern(jax.random.fold_in(key_of[3], 71), 0)
    return dict(sign_iterate=sign_iterate, operand_pattern=operand_pattern, product_pattern=product_pattern)


def expand_blocks(pattern):
    count = pattern.shape[0]
    forced = jnp.maximum(pattern, jnp.eye(count, dtype=jnp.int32)).astype(jnp.float32)
    wide = jnp.broadcast_to(forced[:, None, :, None], (count, BS, count, BS))
    return wide.reshape(count * BS, count * BS)


def reference(sign_iterate, operand_pattern, product_pattern):
    operand_mask = expand_blocks(operand_pattern)
    product_mask = expand_blocks(product_pattern)
    sparse_iterate = sign_iterate * operand_mask
    square = jnp.dot(sparse_iterate, sparse_iterate, precision=lax.Precision.HIGHEST, preferred_element_type=jnp.float32) * product_mask
    identity = jnp.eye(sign_iterate.shape[0], dtype=jnp.float32)
    polynomial = 3.0 * identity - square
    sign_next = 0.5 * jnp.dot(sparse_iterate, polynomial, precision=lax.Precision.HIGHEST, preferred_element_type=jnp.float32) * product_mask
    defect = jnp.sum((square - identity) ** 2)
    return sign_next, defect
```

```python
import functools

import jax
import jax.numpy as jnp
import numpy as np
from jax import lax
from jax.experimental import pallas as pl
from jax.experimental.pallas import tpu as pltpu
from jax.sharding import PartitionSpec as P

BS = 6
AXES = ("row", "col")
LANES = 128
FLAG = 1024.0
SLOTS_X = 42
SLOTS_S = 64
WIDE_X = 256
WIDE_S = 384
EXTRA = 8
VMEM = 56 * 1024 * 1024


def send(value, move):
    pairs = []
    for row in range(16):
        for col in range(8):
            here = (row // 8, row // 2 % 4, row % 2, col // 4, col % 4)
            xh, z, core, xl, y = move(*here)
            pairs.append((row * 8 + col, ((xh % 2) * 8 + (z % 4) * 2 + core % 2) * 8 + (xl % 2) * 4 + y % 4))
    return lax.ppermute(value, AXES, pairs)


def along(xh=0, z=0, core=0, xl=0, y=0):
    return lambda a, b, c, d, e: (a + xh, b + z, c + core, d + xl, e + y)


def tables():
    row_of = np.arange(64 * BS)[:, None] // BS == np.arange(64)[None, :]
    molecule = np.arange(LANES)[:, None]
    lane = np.arange(LANES * BS)[None, :] // BS
    place = BS * (molecule < lane) + FLAG * (molecule == lane)
    until = np.arange(LANES)[:, None] <= np.arange(LANES)[None, :]
    slot_x = BS * (np.arange(LANES)[:, None] == np.arange(WIDE_X)[None, :] // BS)
    slot_s = BS * (np.arange(LANES)[:, None] == np.arange(WIDE_S)[None, :] // BS)
    within = np.broadcast_to(np.arange(LANES * BS) % BS, (8, LANES * BS))
    to = lambda t: jnp.asarray(t.astype(np.float32), jnp.bfloat16)
    return to(row_of), to(place), to(until), to(slot_x), to(slot_s), jnp.asarray(within.astype(np.int32))


def dot(a, b):
    return jnp.dot(a, b, preferred_element_type=jnp.float32)


def take(source, index):
    return jnp.take_along_axis(source, index, axis=1, mode="promise_in_bounds")


def packed_columns(pattern, row_of, until, slot, within):
    bits = pattern.astype(jnp.bfloat16)
    count = dot(bits, until)
    wanted = lax.broadcasted_iota(jnp.int32, count.shape, 1).astype(jnp.float32)
    position = jnp.zeros(count.shape, jnp.int32)
    for step in (64, 32, 16, 8, 4, 2, 1):
        below = take(count, position + (step - 1)) <= wanted
        position = jnp.where(below, position + step, position)
    rows = dot(row_of, position.astype(jnp.float32).astype(jnp.bfloat16))
    width = slot.shape[1]
    columns = dot(rows.astype(jnp.bfloat16), slot).astype(jnp.int32) + within[0:1, :width]
    return columns, jnp.max(count[:, LANES - 1 :])


def pack_rows(source, columns, chunk, width):
    outs = []
    for j in range(width // LANES):
        index = columns[:, j * LANES : (j + 1) * LANES]
        low = index & (LANES - 1)
        high = index >> 7
        value = take(source(j), low)
        for k in range(j + 1, BS):
            value = jnp.where(high == k, take(source(k), low), value)
        outs.append(value)
    return outs


def pack_kernel(x_ref, pattern_ref, row_of_ref, until_ref, slot_ref, within_ref, out_ref, flag_ref, columns_ref):
    pattern = pattern_ref[...]
    columns, most = packed_columns(pattern, row_of_ref[...], until_ref[...], slot_ref[...], within_ref[...])
    columns_ref[...] = columns
    flag_ref[...] = jnp.full(flag_ref.shape, jnp.where(most > SLOTS_X, 1.0, 0.0), jnp.float32)

    def body(i, carry):
        rows = pl.ds(pl.multiple_of(i * 48, 48), 48)
        outs = pack_rows(lambda k: x_ref[rows, k * LANES : (k + 1) * LANES], columns_ref[rows, :], 48, WIDE_X)
        for j, value in enumerate(outs):
            out_ref[rows, j * LANES : (j + 1) * LANES] = value
        return carry

    lax.fori_loop(0, 8, body, 0)
    real = pattern.astype(jnp.float32)
    out_ref[384:416, :LANES] = real[:32]
    out_ref[384:416, LANES:] = real[32:]


def plan_kernel(pattern_ref, row_of_ref, until_ref, slot_ref, within_ref, columns_ref, flag_ref):
    columns, most = packed_columns(pattern_ref[...], row_of_ref[...], until_ref[...], slot_ref[...], within_ref[...])
    columns_ref[...] = columns
    flag_ref[...] = jnp.full(flag_ref.shape, jnp.where(most > SLOTS_S, 1.0, 0.0), jnp.float32)


def codes(pattern, row_of, place):
    rows = dot(row_of, pattern.astype(jnp.bfloat16)).astype(jnp.bfloat16)
    return dot(rows, place)


def unpack(packed_ref, code_ref, within_ref, high_ref, low_ref, width, first):
    def body(i, carry):
        rows = pl.ds(pl.multiple_of(i * 48, 48), 48)
        target = pl.ds(pl.multiple_of(first + i * 48, 48), 48)
        sources = [packed_ref[rows, k * LANES : (k + 1) * LANES] for k in range(width // LANES)]
        for j in range(BS):
            span = slice(j * LANES, (j + 1) * LANES)
            code = code_ref[rows, span]
            index = (code.astype(jnp.int32) + within_ref[0:1, span]) & 1023
            low = index & (LANES - 1)
            value = take(sources[0], low)
            for k in range(1, min(j + 1, len(sources))):
                value = jnp.where(index >= k * LANES, take(sources[k], low), value)
            value = jnp.where(code >= FLAG, value, 0.0)
            high = value.astype(jnp.bfloat16)
            high_ref[target, span] = high
            low_ref[target, span] = (value - high.astype(jnp.float32)).astype(jnp.bfloat16)
        return carry

    lax.fori_loop(0, 8, body, 0)


def carried_pattern(stack_ref, slot):
    return jnp.concatenate([stack_ref[slot, 384:416, :LANES], stack_ref[slot, 384:416, LANES:]], axis=0)


def left_kernel(where_ref, *refs):
    blocks = refs[:8]
    row_of_ref, place_ref, within_ref, high_ref, low_ref, stack_ref, code_ref, sems = refs[8:]
    step = pl.program_id(0)

    @pl.when(step == 0)
    def _():
        for k in range(8):
            pltpu.make_async_copy(blocks[k], stack_ref.at[k], sems.at[k]).start()

    pltpu.make_async_copy(blocks[0], stack_ref.at[step], sems.at[step]).wait()
    code_ref[...] = codes(carried_pattern(stack_ref, step), row_of_ref[...], place_ref[...])
    unpack(stack_ref.at[step], code_ref, within_ref, high_ref.at[0], low_ref.at[0], WIDE_X, 0)


def accumulate(step, left_high_ref, left_low_ref, high_ref, low_ref, total_ref):
    for j in range(3):
        span = slice(j * 256, (j + 1) * 256)
        part = dot(left_high_ref[0], high_ref[:, span]) + dot(left_high_ref[0], low_ref[:, span])
        part = part + dot(left_low_ref[0], high_ref[:, span])

        @pl.when(step == 0)
        def _():
            total_ref[:, span] = part

        @pl.when(step > 0)
        def _():
            total_ref[:, span] += part


def square_kernel(where_ref, *refs):
    blocks = refs[:16]
    left_high_ref, left_low_ref, pattern_ref, columns_ref, row_of_ref, place_ref, within_ref = refs[16:23]
    out_ref, defect_ref, stack_ref, code_ref, high_ref, low_ref, total_ref, sems = refs[23:]
    step = pl.program_id(0)

    @pl.when(step == 0)
    def _():
        for k in range(16):
            slot = where_ref[k]
            pltpu.make_async_copy(blocks[k], stack_ref.at[slot], sems.at[slot]).start()

    for half in range(2):
        slot = 2 * step + half
        pltpu.make_async_copy(blocks[0], stack_ref.at[slot], sems.at[slot]).wait()
        code_ref[...] = codes(carried_pattern(stack_ref, slot), row_of_ref[...], place_ref[...])
        unpack(stack_ref.at[slot], code_ref, within_ref, high_ref, low_ref, WIDE_X, half * 384)
    accumulate(step, left_high_ref, left_low_ref, high_ref, low_ref, total_ref)

    @pl.when(step == 7)
    def _():
        code_ref[...] = codes(pattern_ref[...], row_of_ref[...], place_ref[...])
        row_first = where_ref[16] * 384
        col_first = where_ref[17] * 768

        def body(i, sums):
            rows = pl.ds(pl.multiple_of(i * 48, 48), 48)
            outs = pack_rows(lambda k: total_ref[rows, k * LANES : (k + 1) * LANES], columns_ref[rows, :], 48, WIDE_S)
            for j, value in enumerate(outs):
                out_ref[rows, j * LANES : (j + 1) * LANES] = value
            entry_rows = row_first + i * 48 + lax.broadcasted_iota(jnp.int32, (48, LANES), 0)
            entry_cols = col_first + lax.broadcasted_iota(jnp.int32, (48, LANES), 1)
            for j in range(BS):
                span = slice(j * LANES, (j + 1) * LANES)
                unit = jnp.where(entry_rows == entry_cols + j * LANES, 1.0, 0.0)
                gap = jnp.where(code_ref[rows, span] >= FLAG, total_ref[rows, span] - unit, 0.0)
                sums = sums + gap * gap
            return sums

        sums = lax.fori_loop(0, 8, body, jnp.zeros((48, LANES), jnp.float32))
        defect_ref[...] = jnp.full(defect_ref.shape, jnp.sum(sums), jnp.float32)


def next_kernel(where_ref, *refs):
    blocks = refs[:16]
    patterns_ref, left_high_ref, left_low_ref, x_ref, operand_ref, product_ref, row_of_ref, place_ref, within_ref = refs[16:25]
    out_ref, stack_ref, code_ref, second_ref, high_ref, low_ref, total_ref, sems = refs[25:]
    step = pl.program_id(0)

    @pl.when(step == 0)
    def _():
        for k in range(16):
            slot = where_ref[k]
            pltpu.make_async_copy(blocks[k], stack_ref.at[slot], sems.at[slot]).start()

    for half in range(2):
        slot = 2 * step + half
        pltpu.make_async_copy(blocks[0], stack_ref.at[slot], sems.at[slot]).wait()
        code_ref[...] = codes(patterns_ref[slot], row_of_ref[...], place_ref[...])
        unpack(stack_ref.at[slot], code_ref, within_ref, high_ref, low_ref, WIDE_S, half * 384)
    accumulate(step, left_high_ref, left_low_ref, high_ref, low_ref, total_ref)

    @pl.when(step == 7)
    def _():
        code_ref[...] = codes(product_ref[...], row_of_ref[...], place_ref[...])
        second_ref[...] = codes(operand_ref[...], row_of_ref[...], place_ref[...])

        def body(i, carry):
            rows = pl.ds(pl.multiple_of(i * 48, 48), 48)
            kept = jnp.where(second_ref[rows, :] >= FLAG, x_ref[rows, :], 0.0)
            value = 1.5 * kept - 0.5 * total_ref[rows, :]
            out_ref[rows, :] = jnp.where(code_ref[rows, :] >= FLAG, value, 0.0)
            return carry

        lax.fori_loop(0, 8, body, 0)


ANY = pl.BlockSpec(memory_space=pl.ANY)


def whole(shape):
    return pl.BlockSpec(shape, lambda i, where: (0,) * len(shape))


def params():
    return pltpu.CompilerParams(vmem_limit_bytes=VMEM)


def f32(*shape):
    return jax.ShapeDtypeStruct(shape, jnp.float32)


def pack(x, pattern, row_of, until, slot, within):
    return pl.pallas_call(
        pack_kernel,
        out_shape=(f32(416, WIDE_X), f32(8, LANES)),
        scratch_shapes=[pltpu.VMEM((384, WIDE_X), jnp.int32)],
        compiler_params=params(),
        name="pack",
    )(x, pattern, row_of, until, slot, within)


def plan(pattern, row_of, until, slot, within):
    return pl.pallas_call(
        plan_kernel,
        out_shape=(jax.ShapeDtypeStruct((384, WIDE_S), jnp.int32), f32(8, LANES)),
        compiler_params=params(),
        name="plan",
    )(pattern, row_of, until, slot, within)


def left_parts(where, blocks, row_of, place, within):
    part = pl.BlockSpec((1, 384, 768), lambda i, where: (where[i], 0, 0))
    return pl.pallas_call(
        left_kernel,
        grid_spec=pltpu.PrefetchScalarGridSpec(
            num_scalar_prefetch=1,
            grid=(8,),
            in_specs=[ANY] * 8 + [whole(t.shape) for t in (row_of, place, within)],
            out_specs=[part, part],
            scratch_shapes=[
                pltpu.VMEM((8, 416, WIDE_X), jnp.float32),
                pltpu.VMEM((384, 768), jnp.float32),
                pltpu.SemaphoreType.DMA((8,)),
            ],
        ),
        out_shape=[jax.ShapeDtypeStruct((8, 384, 768), jnp.bfloat16)] * 2,
        compiler_params=params(),
        cost_estimate=pl.CostEstimate(flops=30_000_000_000, bytes_accessed=13_000_000, transcendentals=0),
        name="left_parts",
    )(where, *blocks, row_of, place, within)


def product_scratch(rows, width):
    return [pltpu.VMEM((16, rows, width), jnp.float32), pltpu.VMEM((384, 768), jnp.float32)]


def product_work():
    return [
        pltpu.VMEM((768, 768), jnp.bfloat16),
        pltpu.VMEM((768, 768), jnp.bfloat16),
        pltpu.VMEM((384, 768), jnp.float32),
        pltpu.SemaphoreType.DMA((16,)),
    ]


LEFT = pl.BlockSpec((1, 384, 768), lambda i, where: (i, 0, 0))


def square_of(where, blocks, high, low, pattern, columns, row_of, place, within):
    rest = (pattern, columns, row_of, place, within)
    return pl.pallas_call(
        square_kernel,
        grid_spec=pltpu.PrefetchScalarGridSpec(
            num_scalar_prefetch=1,
            grid=(8,),
            in_specs=[ANY] * 16 + [LEFT, LEFT] + [whole(t.shape) for t in rest],
            out_specs=[whole((384, WIDE_S)), whole((8, WIDE_S))],
            scratch_shapes=product_scratch(416, WIDE_X) + product_work(),
        ),
        out_shape=[f32(384, WIDE_S), f32(8, WIDE_S)],
        compiler_params=params(),
        cost_estimate=pl.CostEstimate(flops=30_000_000_000, bytes_accessed=20_000_000, transcendentals=0),
        name="square",
    )(where, *blocks, high, low, *rest)


def next_of(where, blocks, patterns, high, low, x, operand, product, row_of, place, within):
    rest = (x, operand, product, row_of, place, within)
    return pl.pallas_call(
        next_kernel,
        grid_spec=pltpu.PrefetchScalarGridSpec(
            num_scalar_prefetch=1,
            grid=(8,),
            in_specs=[ANY] * 16 + [whole(patterns.shape), LEFT, LEFT] + [whole(t.shape) for t in rest],
            out_specs=whole((384, 768)),
            scratch_shapes=product_scratch(384, WIDE_S) + [pltpu.VMEM((384, 768), jnp.float32)] + product_work(),
        ),
        out_shape=f32(384, 768),
        compiler_params=params(),
        cost_estimate=pl.CostEstimate(flops=30_000_000_000, bytes_accessed=20_000_000, transcendentals=0),
        name="next_iterate",
    )(where, *blocks, patterns, high, low, *rest)


def column_blocks(own):
    other = send(own, along(xh=1))
    blocks = []
    for t in (own, other):
        blocks += [t, send(t, along(z=1)), send(t, along(z=-1)), send(t, along(z=2))]
    return blocks + [send(t, along(core=1)) for t in blocks]


def column_places():
    row = lax.axis_index("row")
    xh, z, core = row // 8, row // 2 % 4, row % 2
    return [
        ((xh + a) % 2) * 8 + ((z + b) % 4) * 2 + (core + c) % 2
        for c in (0, 1)
        for a in (0, 1)
        for b in (0, 3, 1, 2)
    ]


def row_blocks(own):
    other = send(own, along(xl=1))
    blocks = []
    for t in (own, other):
        blocks += [t, send(t, along(y=1)), send(t, along(y=-1)), send(t, along(y=2))]
    return blocks


def row_places():
    col = lax.axis_index("col")
    xl, y = col // 4, col % 4
    return [((xl + a) % 2) * 4 + (y + b) % 4 for a in (0, 1) for b in (0, 3, 1, 2)]


def expand_blocks(pattern):
    rows, cols = pattern.shape
    wide = jnp.broadcast_to(pattern.astype(jnp.float32)[:, None, :, None], (rows, BS, cols, BS))
    return wide.reshape(rows * BS, cols * BS)


def matmul_high(left, right):
    return jnp.dot(left, right, precision=lax.Precision.HIGHEST, preferred_element_type=jnp.float32)


def full_rows(sign_iterate, operand_pattern, product_pattern):
    local_rows, local_cols = sign_iterate.shape
    product_mask = expand_blocks(product_pattern)
    sparse_iterate = sign_iterate * expand_blocks(operand_pattern)
    entry_rows = lax.axis_index("row") * local_rows + jnp.arange(local_rows, dtype=jnp.int32)
    entry_cols = lax.axis_index("col") * local_cols + jnp.arange(local_cols, dtype=jnp.int32)
    identity = (entry_rows[:, None] == entry_cols[None, :]).astype(jnp.float32)
    left = lax.all_gather(sparse_iterate, "col", axis=1, tiled=True)
    square = matmul_high(left, lax.all_gather(sparse_iterate, "row", axis=0, tiled=True)) * product_mask
    polynomial = 3.0 * identity - square
    sign_next = 0.5 * matmul_high(left, lax.all_gather(polynomial, "row", axis=0, tiled=True)) * product_mask
    defect = lax.psum(jnp.sum((square - identity) ** 2), AXES)
    return sign_next, defect


def per_device(sign_iterate, operand_pattern, product_pattern):
    row_of, place, until, slot_x, slot_s, within = tables()
    packed, flag_x = pack(sign_iterate, operand_pattern, row_of, until, slot_x, within)
    columns, flag_s = plan(product_pattern, row_of, until, slot_s, within)
    here = [lax.axis_index("row"), lax.axis_index("col")]
    right_where = jnp.stack(column_places() + here).astype(jnp.int32)
    left_where = jnp.stack(row_places()).astype(jnp.int32)

    patterns = lax.all_gather(product_pattern, "row", axis=0)
    left = row_blocks(packed)
    right = column_blocks(packed)
    high, low = left_parts(left_where, left, row_of, place, within)
    square, defect_tile = square_of(
        right_where, right, high, low, product_pattern, columns, row_of, place, within
    )

    part = jnp.stack([defect_tile[0, 0], jnp.maximum(flag_x[0, 0], flag_s[0, 0])])
    part = jnp.broadcast_to(part[:, None], (2, LANES))
    for step in (along(core=1), along(xh=1), along(xl=1)):
        part = part + send(part, step)
    for axis in ("z", "y"):
        part = part + send(part, along(**{axis: 2}))
        part = part + send(part, flip(axis))

    right = column_blocks(square)
    sign_next = next_of(
        right_where, right, patterns, high, low, sign_iterate, operand_pattern, product_pattern, row_of, place, within
    )
    return lax.cond(
        part[1, 0] > 0.0,
        lambda: full_rows(sign_iterate, operand_pattern, product_pattern),
        lambda: (sign_next, part[0, 0]),
    )


def flip(axis):
    if axis == "z":
        return lambda a, b, c, d, e: (a, b ^ 1, c, d, e)
    return lambda a, b, c, d, e: (a, b, c, d, e ^ 1)


def solution(mesh):
    spec = P("row", "col")
    return jax.shard_map(
        per_device, mesh=mesh, in_specs=(spec, spec, spec), out_specs=(spec, P()), check_vma=False
    )
```

```python
import jax
import jax.numpy as jnp
from jax import lax
from jax.experimental import pallas as pl
from jax.experimental.pallas import tpu as pltpu
from jax.sharding import PartitionSpec as P

BS = 6
AXES = ("row", "col")
LANES = 128
SLOTS_X = 42
SLOTS_S = 64
WIDE_X = 256
WIDE_S = 384
VMEM = 56 * 1024 * 1024


def send(value, move):
    pairs = []
    for row in range(16):
        for col in range(8):
            here = (row // 8, row // 2 % 4, row % 2, col // 4, col % 4)
            xh, z, core, xl, y = move(*here)
            pairs.append((row * 8 + col, ((xh % 2) * 8 + (z % 4) * 2 + core % 2) * 8 + (xl % 2) * 4 + y % 4))
    return lax.ppermute(value, AXES, pairs)


def along(xh=0, z=0, core=0, xl=0, y=0):
    return lambda a, b, c, d, e: (a + xh, b + z, c + core, d + xl, e + y)


def dot(a, b):
    return jnp.dot(a, b, preferred_element_type=jnp.float32)


def take(source, index):
    return jnp.take_along_axis(source, index, axis=1, mode="promise_in_bounds")


def lanes_of():
    return lax.broadcasted_iota(jnp.int32, (64, LANES), 1)


def counts(bits):
    before = lax.broadcasted_iota(jnp.int32, (LANES, LANES), 0)
    until = (before <= lax.broadcasted_iota(jnp.int32, (LANES, LANES), 1)).astype(jnp.float32)
    return dot(bits.astype(jnp.bfloat16), until.astype(jnp.bfloat16))


def slot_sources(bits, slots):
    count = counts(bits)
    lane = lanes_of()
    group = sum((lane >= slots * k).astype(jnp.int32) for k in range(1, LANES // slots))
    wanted = (lane - group * slots).astype(jnp.float32)
    position = jnp.zeros(count.shape, jnp.int32)
    for step in (64, 32, 16, 8, 4, 2, 1):
        below = take(count, position + (step - 1)) <= wanted
        position = jnp.where(below, position + step, position)
    return position, group, jnp.max(count[:, LANES - 1 :])


def flag_of(most, slots):
    return jnp.full((8, LANES), jnp.where(most > slots, 1.0, 0.0), jnp.float32)


def pack_kernel(x_ref, pattern_ref, out_ref, flag_ref, tall_ref):
    for k in range(BS):
        tall_ref[k * 384 : (k + 1) * 384, :] = x_ref[:, k * LANES : (k + 1) * LANES]
    bits = pattern_ref[...].astype(jnp.float32)
    position, group, most = slot_sources(bits, SLOTS_X)
    flag_ref[...] = flag_of(most, SLOTS_X)
    used = lanes_of() < 3 * SLOTS_X
    for t in range(2):
        column = position * BS + (group + 3 * t)
        column = jnp.where(used, column, 0)
        low, high = column & (LANES - 1), column >> 7
        for b in range(BS):
            value = jnp.zeros((64, LANES), jnp.float32)
            for k in range(BS):
                source = tall_ref[pl.ds(k * 384 + b, 64, stride=BS), :]
                value = jnp.where(high == k, take(source, low), value)
            out_ref[b * 64 : (b + 1) * 64, t * LANES : (t + 1) * LANES] = jnp.where(used, value, 0.0)
    out_ref[384:416, :LANES] = bits[:32]
    out_ref[384:416, LANES:] = bits[32:]


def split(value):
    high = value.astype(jnp.bfloat16)
    return high, (value - high.astype(jnp.float32)).astype(jnp.bfloat16)


def unpack_steps(packed_ref, bits, slots, put):
    per = LANES // slots
    present = bits > 0.5
    rank = (counts(bits) - bits).astype(jnp.int32)
    spare = per * slots < LANES
    if spare:
        index = [jnp.where(present, rank + slots * k, LANES - 1) for k in range(per)]
    else:
        index = [jnp.minimum(rank + slots * k, LANES - 1) for k in range(per)]

    def one(b):
        def run():
            for c in range(BS):
                source = packed_ref[b * 64 : (b + 1) * 64, c // per * LANES : (c // per + 1) * LANES]
                value = take(source, index[c % per])
                if not spare:
                    value = jnp.where(present, value, 0.0)
                put(b, c, *split(value))

        return run

    return [one(b) for b in range(BS)]


def carried(packed_ref):
    return jnp.concatenate([packed_ref[384:416, :LANES], packed_ref[384:416, LANES:]], axis=0)


def left_kernel(where_ref, *refs):
    blocks = refs[:8]
    high_ref, low_ref, stack_ref, sems = refs[8:]
    step = pl.program_id(0)

    @pl.when(step == 0)
    def _():
        for k in range(8):
            pltpu.make_async_copy(blocks[k], stack_ref.at[k], sems.at[k]).start()

    pltpu.make_async_copy(blocks[0], stack_ref.at[step], sems.at[step]).wait()

    def put(b, c, high, low):
        high_ref[0, b * 64 : (b + 1) * 64, c * LANES : (c + 1) * LANES] = high
        low_ref[0, b * 64 : (b + 1) * 64, c * LANES : (c + 1) * LANES] = low

    packed_ref = stack_ref.at[step]
    for run in unpack_steps(packed_ref, carried(packed_ref), SLOTS_X, put):
        run()


def unpack_pair(stack_ref, bits_of, slots, pair, high_ref, low_ref):
    steps = []
    for half in range(2):
        first = half * 64

        def put(b, c, high, low, first=first):
            rows = slice(b * 128 + first, b * 128 + first + 64)
            high_ref[rows, c * LANES : (c + 1) * LANES] = high
            low_ref[rows, c * LANES : (c + 1) * LANES] = low

        slot = 2 * pair + half
        steps += unpack_steps(stack_ref.at[slot], bits_of(slot), slots, put)
    return steps


def multiply(left_high_ref, left_low_ref, at, high_ref, low_ref, total_ref, others):
    for j in range(3):
        for run in others[4 * j : 4 * j + 4]:
            run()
        span = slice(j * 256, (j + 1) * 256)
        part = dot(left_high_ref[at], high_ref[:, span]) + dot(left_high_ref[at], low_ref[:, span])
        total_ref[:, span] += part + dot(left_low_ref[at], high_ref[:, span])


def product(where_ref, blocks, bits_of, slots, left_high_ref, left_low_ref, stack_ref, work, finish):
    high_a, low_a, high_b, low_b, total_ref, sems = work
    step = pl.program_id(0)

    def arrived(pair):
        for half in range(2):
            slot = 2 * pair + half
            pltpu.make_async_copy(blocks[0], stack_ref.at[slot], sems.at[slot]).wait()

    @pl.when(step == 0)
    def _():
        for k in range(16):
            slot = column_place(where_ref, k)
            pltpu.make_async_copy(blocks[k], stack_ref.at[slot], sems.at[slot]).start()
        total_ref[...] = jnp.zeros_like(total_ref)
        arrived(0)
        for run in unpack_pair(stack_ref, bits_of, slots, 0, high_a, low_a):
            run()

    arrived(2 * step + 1)
    others = unpack_pair(stack_ref, bits_of, slots, 2 * step + 1, high_b, low_b)
    multiply(left_high_ref, left_low_ref, 0, high_a, low_a, total_ref, others)

    @pl.when(step < 3)
    def _():
        arrived(2 * step + 2)
        others = unpack_pair(stack_ref, bits_of, slots, 2 * step + 2, high_a, low_a)
        multiply(left_high_ref, left_low_ref, 1, high_b, low_b, total_ref, others)

    @pl.when(step == 3)
    def _():
        multiply(left_high_ref, left_low_ref, 1, high_b, low_b, total_ref, [])
        finish(total_ref)


def square_kernel(where_ref, *refs):
    blocks = refs[:16]
    left_high_ref, left_low_ref, pattern_ref = refs[16:19]
    out_ref, defect_ref, flag_ref, stack_ref = refs[19:23]

    def finish(total_ref):
        bits = pattern_ref[...].astype(jnp.float32)
        present = bits > 0.5
        position, group, most = slot_sources(bits, SLOTS_S)
        flag_ref[...] = flag_of(most, SLOTS_S)
        first_rows = where_ref[0] * 64 + lax.broadcasted_iota(jnp.int32, (64, LANES), 0)
        unit = jnp.where(first_rows == where_ref[1] * LANES + lanes_of(), 1.0, 0.0)
        position = jnp.minimum(position, LANES - 1)
        sums = jnp.zeros((64, LANES), jnp.float32)
        for b in range(BS):
            rows = slice(b * 64, (b + 1) * 64)
            for t in range(3):
                values = []
                for c in (2 * t, 2 * t + 1):
                    square = total_ref[rows, c * LANES : (c + 1) * LANES]
                    gap = jnp.where(present, square - unit if b == c else square, 0.0)
                    sums = sums + gap * gap
                    values.append(take(3.0 * unit - square if b == c else -square, position))
                out_ref[rows, t * LANES : (t + 1) * LANES] = jnp.where(group == 0, values[0], values[1])
        defect_ref[...] = jnp.full(defect_ref.shape, jnp.sum(sums), jnp.float32)

    product(
        where_ref, blocks, lambda slot: carried(stack_ref.at[slot]), SLOTS_X,
        left_high_ref, left_low_ref, stack_ref, refs[23:], finish,
    )


def next_kernel(where_ref, *refs):
    blocks = refs[:16]
    patterns_ref, left_high_ref, left_low_ref, pattern_ref = refs[16:20]
    out_ref, stack_ref, tall_ref = refs[20:23]

    def finish(total_ref):
        present = pattern_ref[...] > 0
        for j in range(BS):
            lane = lanes_of() + j * LANES
            molecule = (lane * 10923) >> 16
            function = lane - molecule * BS
            for b in range(BS):
                value = jnp.zeros((64, LANES), jnp.float32)
                for c in range(BS):
                    source = total_ref[b * 64 : (b + 1) * 64, c * LANES : (c + 1) * LANES]
                    source = jnp.where(present, 0.5 * source, 0.0)
                    value = jnp.where(function == c, take(source, molecule), value)
                tall_ref[pl.ds(j * 384 + b, 64, stride=BS), :] = value
            out_ref[:, j * LANES : (j + 1) * LANES] = tall_ref[j * 384 : (j + 1) * 384, :]

    product(
        where_ref, blocks, lambda slot: patterns_ref[slot], SLOTS_S,
        left_high_ref, left_low_ref, stack_ref, refs[23:], finish,
    )


ANY = pl.BlockSpec(memory_space=pl.ANY)


def whole(shape):
    return pl.BlockSpec(shape, lambda i, where: (0,) * len(shape))


def params():
    return pltpu.CompilerParams(vmem_limit_bytes=VMEM)


def f32(*shape):
    return jax.ShapeDtypeStruct(shape, jnp.float32)


def cost(us):
    return pl.CostEstimate(flops=int(us * 1_000_000_000), bytes_accessed=int(us * 500_000), transcendentals=0)


def pack(x, pattern):
    return pl.pallas_call(
        pack_kernel,
        out_shape=(f32(416, WIDE_X), f32(8, LANES)),
        scratch_shapes=[pltpu.VMEM((BS * 384, LANES), jnp.float32)],
        compiler_params=params(),
        name="pack",
    )(x, pattern)


def left_parts(where, blocks):
    part = pl.BlockSpec((1, 384, 768), lambda i, where: (row_place(where, i), 0, 0))
    return pl.pallas_call(
        left_kernel,
        grid_spec=pltpu.PrefetchScalarGridSpec(
            num_scalar_prefetch=1,
            grid=(8,),
            in_specs=[ANY] * 8,
            out_specs=[part, part],
            scratch_shapes=[pltpu.VMEM((8, 416, WIDE_X), jnp.float32), pltpu.SemaphoreType.DMA((8,))],
        ),
        out_shape=[jax.ShapeDtypeStruct((8, 384, 768), jnp.bfloat16)] * 2,
        compiler_params=params(),
        cost_estimate=cost(8),
        name="left_parts",
    )(where, *blocks)


def product_work():
    return [pltpu.VMEM((768, 768), jnp.bfloat16)] * 4 + [
        pltpu.VMEM((384, 768), jnp.float32),
        pltpu.SemaphoreType.DMA((16,)),
    ]


LEFT = pl.BlockSpec((2, 384, 768), lambda i, where: (i, 0, 0))


def square_of(where, blocks, high, low, pattern):
    return pl.pallas_call(
        square_kernel,
        grid_spec=pltpu.PrefetchScalarGridSpec(
            num_scalar_prefetch=1,
            grid=(4,),
            in_specs=[ANY] * 16 + [LEFT, LEFT, whole(pattern.shape)],
            out_specs=[whole((384, WIDE_S)), whole((8, LANES)), whole((8, LANES))],
            scratch_shapes=[pltpu.VMEM((16, 416, WIDE_X), jnp.float32)] + product_work(),
        ),
        out_shape=[f32(384, WIDE_S), f32(8, LANES), f32(8, LANES)],
        compiler_params=params(),
        cost_estimate=cost(25),
        name="square",
    )(where, *blocks, high, low, pattern)


def next_of(where, blocks, patterns, high, low, pattern):
    return pl.pallas_call(
        next_kernel,
        grid_spec=pltpu.PrefetchScalarGridSpec(
            num_scalar_prefetch=1,
            grid=(4,),
            in_specs=[ANY] * 16 + [whole(patterns.shape), LEFT, LEFT, whole(pattern.shape)],
            out_specs=whole((384, 768)),
            scratch_shapes=[pltpu.VMEM((16, 384, WIDE_S), jnp.float32), pltpu.VMEM((BS * 384, LANES), jnp.float32)]
            + product_work(),
        ),
        out_shape=f32(384, 768),
        compiler_params=params(),
        cost_estimate=cost(25),
        name="next_iterate",
    )(where, *blocks, patterns, high, low, pattern)


def column_blocks(own):
    other = send(own, along(xh=1))
    blocks = []
    for t in (own, other):
        blocks += [t, send(t, along(z=1)), send(t, along(z=-1)), send(t, along(z=2))]
    return blocks + [send(t, along(core=1)) for t in blocks]


def column_place(where_ref, k):
    row = where_ref[0]
    a, b, c = k // 4 % 2, (0, 3, 1, 2)[k % 4], k // 8
    return ((row >> 3) ^ a) * 8 + (((row >> 1) + b) & 3) * 2 + ((row & 1) ^ c)


def row_blocks(own):
    other = send(own, along(xl=1))
    blocks = []
    for t in (own, other):
        blocks += [t, send(t, along(y=1)), send(t, along(y=-1)), send(t, along(y=2))]
    return blocks


def row_place(where_ref, k):
    col = where_ref[1]
    place = k & 3
    b = jnp.where(place == 0, 0, jnp.where(place == 1, 3, place - 1))
    return ((col >> 2) ^ (k >> 2)) * 4 + ((col + b) & 3)


def expand_blocks(pattern):
    rows, cols = pattern.shape
    wide = jnp.broadcast_to(pattern.astype(jnp.float32)[:, None, :, None], (rows, BS, cols, BS))
    return wide.reshape(rows * BS, cols * BS)


def matmul_high(left, right):
    return jnp.dot(left, right, precision=lax.Precision.HIGHEST, preferred_element_type=jnp.float32)


def full_rows(sign_iterate, operand_pattern, product_pattern):
    local_rows, local_cols = sign_iterate.shape
    product_mask = expand_blocks(product_pattern)
    sparse_iterate = sign_iterate * expand_blocks(operand_pattern)
    entry_rows = lax.axis_index("row") * local_rows + jnp.arange(local_rows, dtype=jnp.int32)
    entry_cols = lax.axis_index("col") * local_cols + jnp.arange(local_cols, dtype=jnp.int32)
    identity = (entry_rows[:, None] == entry_cols[None, :]).astype(jnp.float32)
    left = lax.all_gather(sparse_iterate, "col", axis=1, tiled=True)
    square = matmul_high(left, lax.all_gather(sparse_iterate, "row", axis=0, tiled=True)) * product_mask
    polynomial = 3.0 * identity - square
    sign_next = 0.5 * matmul_high(left, lax.all_gather(polynomial, "row", axis=0, tiled=True)) * product_mask
    defect = lax.psum(jnp.sum((square - identity) ** 2), AXES)
    return sign_next, defect


def after(value, *earlier):
    return lax.optimization_barrier((value, *earlier))[0]


def per_device(sign_iterate, operand_pattern, product_pattern):
    patterns = lax.all_gather(product_pattern.astype(jnp.float32), "row", axis=0)
    packed, flag_x = pack(sign_iterate, operand_pattern)
    where = jnp.stack([lax.axis_index("row"), lax.axis_index("col")]).astype(jnp.int32)

    left = row_blocks(packed)
    right = column_blocks(packed)
    high, low = left_parts(where, left)
    square, part, flag_s = square_of(where, right, high, low, product_pattern)
    part = jnp.concatenate([part, jnp.maximum(flag_x, flag_s)])

    right = column_blocks(square)
    moves = [along(core=1), along(xh=1), along(xl=1), along(z=2), flip("z"), along(y=2), flip("y")]
    for move, bulk in zip(moves, right[1:8]):
        part = after(part, bulk)
        part = part + send(part, move)

    sign_next = next_of(where, right, patterns, high, low, product_pattern)
    return lax.cond(
        part[8, 0] > 0.0,
        lambda: full_rows(sign_iterate, operand_pattern, product_pattern),
        lambda: (sign_next, part[0, 0]),
    )


def flip(axis):
    if axis == "z":
        return lambda a, b, c, d, e: (a, b ^ 1, c, d, e)
    return lambda a, b, c, d, e: (a, b, c, d, e ^ 1)


def solution(mesh):
    spec = P("row", "col")
    return jax.shard_map(
        per_device, mesh=mesh, in_specs=(spec, spec, spec), out_specs=(spec, P()), check_vma=False
    )
```

```python
import functools

import jax
import jax.numpy as jnp
from jax import lax
from jax.experimental import pallas as pl
from jax.experimental.pallas import tpu as pltpu
from jax.sharding import PartitionSpec as P

BS = 6
AXES = ("row", "col")
LANES = 128
SLOTS_X = 42
SLOTS_S = 64
WIDE_X = 256
WIDE_S = 384
VMEM = 26 * 1024 * 1024


def send(value, move):
    pairs = []
    for row in range(16):
        for col in range(8):
            here = (row // 8, row // 2 % 4, row % 2, col // 4, col % 4)
            xh, z, core, xl, y = move(*here)
            pairs.append((row * 8 + col, ((xh % 2) * 8 + (z % 4) * 2 + core % 2) * 8 + (xl % 2) * 4 + y % 4))
    return lax.ppermute(value, AXES, pairs)


def along(xh=0, z=0, core=0, xl=0, y=0):
    return lambda a, b, c, d, e: (a + xh, b + z, c + core, d + xl, e + y)


def dot(a, b):
    return jnp.dot(a, b, preferred_element_type=jnp.float32)


def take(source, index):
    return jnp.take_along_axis(source, index, axis=1, mode="promise_in_bounds")


def lanes_of():
    return lax.broadcasted_iota(jnp.int32, (64, LANES), 1)


def counts(bits):
    before = lax.broadcasted_iota(jnp.int32, (LANES, LANES), 0)
    until = (before <= lax.broadcasted_iota(jnp.int32, (LANES, LANES), 1)).astype(jnp.float32)
    return dot(bits.astype(jnp.bfloat16), until.astype(jnp.bfloat16))


def slot_sources(bits, slots):
    count = counts(bits)
    lane = lanes_of()
    group = sum((lane >= slots * k).astype(jnp.int32) for k in range(1, LANES // slots))
    wanted = (lane - group * slots).astype(jnp.float32)
    position = jnp.zeros(count.shape, jnp.int32)
    for step in (64, 32, 16, 8, 4, 2, 1):
        below = take(count, position + (step - 1)) <= wanted
        position = jnp.where(below, position + step, position)
    return position, group, jnp.max(count[:, LANES - 1 :])


def flag_of(most, slots):
    return jnp.full((8, LANES), jnp.where(most > slots, 1.0, 0.0), jnp.float32)


def pack_kernel(x_ref, pattern_ref, product_ref, left_ref, right_ref, flag_ref, tall_ref):
    for k in range(BS):
        tall_ref[k * 384 : (k + 1) * 384, :] = x_ref[:, k * LANES : (k + 1) * LANES]
    bits = pattern_ref[...].astype(jnp.float32)
    position, group, most = slot_sources(bits, SLOTS_X)
    flag_ref[...] = flag_of(most, SLOTS_X)
    used = lanes_of() < 3 * SLOTS_X
    for t in range(2):
        column = position * BS + (group + 3 * t)
        column = jnp.where(used, column, 0)
        low, high = column & (LANES - 1), column >> 7
        for b in range(BS):
            value = jnp.zeros((64, LANES), jnp.float32)
            for k in range(BS):
                source = tall_ref[pl.ds(k * 384 + b, 64, stride=BS), :]
                value = jnp.where(high == k, take(source, low), value)
            value = jnp.where(used, value, 0.0)
            for out_ref in (left_ref, right_ref):
                out_ref[b * 64 : (b + 1) * 64, t * LANES : (t + 1) * LANES] = value
    product = product_ref[...].astype(jnp.float32)
    for out_ref, first, source in ((left_ref, 384, bits), (right_ref, 384, bits), (right_ref, 416, product)):
        out_ref[first : first + 32, :LANES] = source[:32]
        out_ref[first : first + 32, LANES:] = source[32:]


def split(value):
    high = value.astype(jnp.bfloat16)
    return high, (value - high.astype(jnp.float32)).astype(jnp.bfloat16)


def unpack_steps(packed_ref, bits, slots, put):
    per = LANES // slots
    present = bits > 0.5
    rank = (counts(bits) - bits).astype(jnp.int32)
    spare = per * slots < LANES
    index = jnp.where(present, rank, LANES - 1) if spare else jnp.minimum(rank, slots - 1)

    def one(q, k):
        def run():
            for t in range(BS // per):
                for b in range(BS):
                    parts = []
                    for r in (16 * q, 16 * q + 8):
                        where = index[r : r + 8] + slots * k
                        if spare:
                            where = jnp.minimum(where, LANES - 1)
                        source = packed_ref[b * 64 + r : b * 64 + r + 8, t * LANES : (t + 1) * LANES]
                        value = take(source, where)
                        if not spare:
                            value = jnp.where(present[r : r + 8], value, 0.0)
                        parts.append(value)
                    put(b, t * per + k, 16 * q, *split(jnp.concatenate(parts, axis=0)))

        return run

    return [one(q, k) for q in range(4) for k in range(per)]


def carried(packed_ref, first):
    rows = slice(first, first + 32)
    return jnp.concatenate([packed_ref[rows, :LANES], packed_ref[rows, LANES:]], axis=0)


def fetch(source_ref, target_ref):
    target_ref[...] = source_ref[...]


def left_kernel(where_ref, *refs):
    blocks = refs[:4]
    high_ref, low_ref, stack_ref = refs[-3:]
    step = pl.program_id(0)

    for k in range(4):
        pl.when(step == k)(functools.partial(fetch, blocks[k], stack_ref))

    def put(b, c, r, high, low):
        rows = slice(b * 64 + r, b * 64 + r + 16)
        high_ref[0, rows, c * LANES : (c + 1) * LANES] = high
        low_ref[0, rows, c * LANES : (c + 1) * LANES] = low

    for run in unpack_steps(stack_ref, carried(stack_ref, 384), SLOTS_X, put):
        run()


def unpack_pair(stack_ref, bits, slots, core, high_ref, low_ref):
    steps = []
    for other in range(2):
        first = (core ^ other) * 64

        def put(b, c, r, high, low, first=first):
            rows = pl.ds(pl.multiple_of(first + (b * 128 + r), 16), 16)
            high_ref[rows, c * LANES : (c + 1) * LANES] = high
            low_ref[rows, c * LANES : (c + 1) * LANES] = low

        steps += unpack_steps(stack_ref.at[other], bits[other], slots, put)
    return steps


def multiply(left_high_ref, left_low_ref, high_ref, low_ref, total_ref, others):
    each = len(others) // 3
    for j in range(3):
        for run in others[each * j : each * (j + 1) if j < 2 else None]:
            run()
        span = slice(j * 256, (j + 1) * 256)
        part = dot(left_high_ref[0], high_ref[:, span]) + dot(left_high_ref[0], low_ref[:, span])
        total_ref[:, span] += part + dot(left_low_ref[0], high_ref[:, span])


def product(where_ref, blocks, bits_of, slots, lefts, work, begin, finish):
    stack_a, stack_b, high_a, low_a, high_b, low_b, total_ref = work
    step = pl.program_id(0)
    pairs = len(blocks) // 2
    last = pairs // 2 - 1
    core = where_ref[0] & 1

    def fetch_pair(pair, stack_ref):
        for other in range(2):
            fetch(blocks[pair + pairs * other], stack_ref.at[other])

    def unpack(pair, stack_ref, high_ref, low_ref):
        bits = [bits_of(2 * pair + other, stack_ref.at[other]) for other in range(2)]
        return unpack_pair(stack_ref, bits, slots, core, high_ref, low_ref)

    @pl.when(step == 0)
    def _():
        begin(total_ref)
        fetch_pair(0, stack_a)
        for run in unpack(0, stack_a, high_a, low_a):
            run()

    for k in range(last + 1):
        pl.when(step == k)(functools.partial(fetch_pair, 2 * k + 1, stack_b))

    multiply(*lefts[:2], high_a, low_a, total_ref, unpack(2 * step + 1, stack_b, high_b, low_b))

    for k in range(last):
        pl.when(step == k)(functools.partial(fetch_pair, 2 * k + 2, stack_a))

    @pl.when(step < last)
    def _():
        multiply(*lefts[2:], high_b, low_b, total_ref, unpack(2 * step + 2, stack_a, high_a, low_a))

    @pl.when(step == last)
    def _():
        multiply(*lefts[2:], high_b, low_b, total_ref, [])
        finish(total_ref)


def zero(total_ref):
    total_ref[...] = jnp.zeros_like(total_ref)


def square_kernel(where_ref, *refs):
    blocks, lefts = refs[:16], refs[16:20]
    pattern_ref, flag_x_ref = refs[20:22]
    out_ref, near_ref, away_ref = refs[22:25]

    def finish(total_ref):
        bits = pattern_ref[...].astype(jnp.float32)
        present = bits > 0.5
        position, group, most = slot_sources(bits, SLOTS_S)
        first_rows = where_ref[0] * 64 + lax.broadcasted_iota(jnp.int32, (64, LANES), 0)
        unit = jnp.where(first_rows == where_ref[1] * LANES + lanes_of(), 1.0, 0.0)
        position = jnp.minimum(position, LANES - 1)
        sums = jnp.zeros((64, LANES), jnp.float32)
        for b in range(BS):
            rows = slice(b * 64, (b + 1) * 64)
            for t in range(3):
                values = []
                for c in (2 * t, 2 * t + 1):
                    square = total_ref[rows, c * LANES : (c + 1) * LANES]
                    gap = jnp.where(present, square - unit if b == c else square, 0.0)
                    sums = sums + gap * gap
                    values.append(take(3.0 * unit - square if b == c else -square, position))
                out_ref[rows, t * LANES : (t + 1) * LANES] = jnp.where(group == 0, values[0], values[1])
        flag = jnp.maximum(flag_of(most, SLOTS_S), flag_x_ref[...])
        out_ref[384:392, :LANES] = jnp.full((8, LANES), jnp.sum(sums), jnp.float32)
        out_ref[384:392, LANES : 2 * LANES] = flag
        out_ref[384:392, 2 * LANES :] = flag
        for k, block_ref in enumerate(blocks):
            kept_ref = (near_ref, away_ref)[k // 4 % 2]
            kept_ref[2 * (k % 4) + k // 8] = carried(block_ref, 416)

    bits_of = lambda slot, packed_ref: carried(packed_ref, 384)
    product(where_ref, blocks, bits_of, SLOTS_X, lefts, refs[25:], zero, finish)


def first_next_kernel(where_ref, *refs):
    blocks, lefts = refs[:8], refs[8:12]
    patterns_ref, out_ref = refs[12:14]

    def finish(total_ref):
        out_ref[...] = total_ref[...]

    product(where_ref, blocks, lambda slot, packed_ref: patterns_ref[slot], SLOTS_S, lefts, refs[14:], zero, finish)


def next_kernel(where_ref, *refs):
    blocks, lefts = refs[:8], refs[8:12]
    patterns_ref, before_ref, pattern_ref = refs[12:15]
    out_ref, tall_ref = refs[15:17]

    def begin(total_ref):
        total_ref[...] = before_ref[...]

    def finish(total_ref):
        present = pattern_ref[...] > 0
        for j in range(BS):
            lane = lanes_of() + j * LANES
            molecule = (lane * 10923) >> 16
            function = lane - molecule * BS
            for b in range(BS):
                value = jnp.zeros((64, LANES), jnp.float32)
                for c in range(BS):
                    source = total_ref[b * 64 : (b + 1) * 64, c * LANES : (c + 1) * LANES]
                    source = jnp.where(present, 0.5 * source, 0.0)
                    value = jnp.where(function == c, take(source, molecule), value)
                tall_ref[pl.ds(j * 384 + b, 64, stride=BS), :] = value
            out_ref[:, j * LANES : (j + 1) * LANES] = tall_ref[j * 384 : (j + 1) * 384, :]

    product(where_ref, blocks, lambda slot, packed_ref: patterns_ref[slot], SLOTS_S, lefts, refs[17:], begin, finish)


ANY = pl.BlockSpec(memory_space=pl.ANY)
HELD = pl.BlockSpec(memory_space=pltpu.VMEM)


def whole(shape):
    return pl.BlockSpec(shape, lambda i, where: (0,) * len(shape))


def params():
    return pltpu.CompilerParams(vmem_limit_bytes=VMEM)


def f32(*shape):
    return jax.ShapeDtypeStruct(shape, jnp.float32)


def cost(us):
    return pl.CostEstimate(flops=int(us * 1_000_000_000), bytes_accessed=int(us * 500_000), transcendentals=0)


def pack(x, operand, product):
    return pl.pallas_call(
        pack_kernel,
        out_shape=(f32(416, WIDE_X), f32(448, WIDE_X), f32(8, LANES)),
        scratch_shapes=[pltpu.VMEM((BS * 384, LANES), jnp.float32)],
        compiler_params=params(),
        name="pack",
    )(x, operand, product)


def left_parts(where, blocks, second, earlier=()):
    part = pl.BlockSpec((1, 384, 768), lambda i, where: (row_place(where, i + 4 * second), 0, 0))
    return pl.pallas_call(
        left_kernel,
        grid_spec=pltpu.PrefetchScalarGridSpec(
            num_scalar_prefetch=1,
            grid=(4,),
            in_specs=[HELD] * 4 + [ANY] * len(earlier),
            out_specs=[part, part],
            scratch_shapes=[pltpu.VMEM((416, WIDE_X), jnp.float32)],
        ),
        out_shape=[jax.ShapeDtypeStruct((8, 384, 768), jnp.bfloat16)] * 2,
        input_output_aliases={5 + k: k for k in range(len(earlier))},
        compiler_params=params(),
        cost_estimate=cost(5),
        name="left_parts",
    )(where, *blocks, *earlier)


def product_call(kernel, name, where, blocks, second, high, low, rest, outs, stack, scratch=()):
    pairs = len(blocks) // 2
    even = pl.BlockSpec((1, 384, 768), lambda i, where: (column_pair(where, second + i // 2, i % 2), 0, 0))
    odd = pl.BlockSpec((1, 384, 768), lambda i, where: (column_pair(where, second + i // 2, 3 - i % 2), 0, 0))
    return pl.pallas_call(
        kernel,
        grid_spec=pltpu.PrefetchScalarGridSpec(
            num_scalar_prefetch=1,
            grid=(pairs // 2,),
            in_specs=[HELD] * len(blocks) + [even, even, odd, odd] + [whole(t.shape) for t in rest],
            out_specs=[whole(shape) for shape in outs],
            scratch_shapes=[*scratch]
            + [pltpu.VMEM((2, *stack), jnp.float32)] * 2
            + [pltpu.VMEM((768, 768), jnp.bfloat16)] * 4
            + [pltpu.VMEM((384, 768), jnp.float32)],
        ),
        out_shape=[f32(*shape) for shape in outs],
        compiler_params=params(),
        cost_estimate=cost(2.5 * pairs),
        name=name,
    )(where, *blocks, high, low, high, low, *rest)


def after(value, *earlier):
    return lax.optimization_barrier((value, *earlier))[0]


GATES = {"U": ("H",), "u": ("l",), "D": ("F",), "d": ("f",)}
GATES_S = {"C": ("U",), "CH": ("F",)}


def run_moves(table, gates, done):
    def get(name):
        if name not in done:
            source, move = table[name]
            value = get(source)
            if name in gates:
                value = after(value, *(get(g) for g in gates[name]))
            done[name] = send(value, move)
        return done[name]

    for name in table:
        get(name)
    return done


def both_blocks(left, right):
    table = dict([
        ("H", ("R", along(xh=1))),
        ("l", ("L", along(xl=1))),
        ("U", ("R", along(z=1))),
        ("u", ("L", along(y=1))),
        ("D", ("R", along(z=-1))),
        ("d", ("L", along(y=-1))),
        ("F", ("R", along(z=2))),
        ("f", ("L", along(y=2))),
        ("C", ("R", along(core=1))),
        ("HU", ("H", along(z=1))),
        ("lu", ("l", along(y=1))),
        ("HD", ("H", along(z=-1))),
        ("ld", ("l", along(y=-1))),
        ("HF", ("F", along(xh=1))),
        ("lf", ("f", along(xl=1))),
        ("CU", ("U", along(core=1))),
        ("CD", ("D", along(core=1))),
        ("CF", ("F", along(core=1))),
        ("CH", ("H", along(core=1))),
        ("CHU", ("HU", along(core=1))),
        ("CHD", ("HD", along(core=1))),
        ("CHF", ("HF", along(core=1))),
    ])
    done = run_moves(table, GATES, {"R": right, "L": left})
    near = [done[k] for k in ("R", "U", "D", "F", "C", "CU", "CD", "CF")]
    away = [done[k] for k in ("H", "HU", "HD", "HF", "CH", "CHU", "CHD", "CHF")]
    row = [done[k] for k in ("L", "u", "d", "f", "l", "lu", "ld", "lf")]
    return row, near, away


def column_blocks(own):
    table = dict([
        ("U", ("R", along(z=1))),
        ("D", ("R", along(z=-1))),
        ("H", ("R", along(xh=1))),
        ("F", ("R", along(z=2))),
        ("C", ("R", along(core=1))),
        ("HU", ("H", along(z=1))),
        ("HD", ("H", along(z=-1))),
        ("CU", ("U", along(core=1))),
        ("CD", ("D", along(core=1))),
        ("CH", ("H", along(core=1))),
        ("HF", ("F", along(xh=1))),
        ("CF", ("F", along(core=1))),
        ("CHU", ("HU", along(core=1))),
        ("CHD", ("HD", along(core=1))),
        ("CHF", ("HF", along(core=1))),
    ])
    done = run_moves(table, GATES_S, {"R": own})
    near = [done[k] for k in ("R", "U", "D", "F", "C", "CU", "CD", "CF")]
    away = [done[k] for k in ("H", "HU", "HD", "HF", "CH", "CHU", "CHD", "CHF")]
    return near, away


def column_pair(where, second, b):
    row = where[0]
    return ((row >> 3) ^ second) * 4 + (((row >> 1) + b) & 3)


def row_place(where_ref, k):
    col = where_ref[1]
    place = k & 3
    b = jnp.where(place == 0, 0, jnp.where(place == 1, 3, place - 1))
    return ((col >> 2) ^ (k >> 2)) * 4 + ((col + b) & 3)


def expand_blocks(pattern):
    rows, cols = pattern.shape
    wide = jnp.broadcast_to(pattern.astype(jnp.float32)[:, None, :, None], (rows, BS, cols, BS))
    return wide.reshape(rows * BS, cols * BS)


def matmul_high(left, right):
    return jnp.dot(left, right, precision=lax.Precision.HIGHEST, preferred_element_type=jnp.float32)


def full_rows(sign_iterate, operand_pattern, product_pattern):
    local_rows, local_cols = sign_iterate.shape
    product_mask = expand_blocks(product_pattern)
    sparse_iterate = sign_iterate * expand_blocks(operand_pattern)
    entry_rows = lax.axis_index("row") * local_rows + jnp.arange(local_rows, dtype=jnp.int32)
    entry_cols = lax.axis_index("col") * local_cols + jnp.arange(local_cols, dtype=jnp.int32)
    identity = (entry_rows[:, None] == entry_cols[None, :]).astype(jnp.float32)
    left = lax.all_gather(sparse_iterate, "col", axis=1, tiled=True)
    square = matmul_high(left, lax.all_gather(sparse_iterate, "row", axis=0, tiled=True)) * product_mask
    polynomial = 3.0 * identity - square
    sign_next = 0.5 * matmul_high(left, lax.all_gather(polynomial, "row", axis=0, tiled=True)) * product_mask
    defect = lax.psum(jnp.sum((square - identity) ** 2), AXES)
    return sign_next, defect


def sum_of(blocks):
    own, up, down, far = (a[384:385, :256] + b[384:385, :256] for a, b in zip(blocks[:4], blocks[4:]))
    return (own + far) + (up + down)


def per_device(sign_iterate, operand_pattern, product_pattern):
    left, right, flag_x = pack(sign_iterate, operand_pattern, product_pattern)
    where = jnp.stack([lax.axis_index("row"), lax.axis_index("col")]).astype(jnp.int32)
    row, near, away = both_blocks(left, right)
    high, low = left_parts(where, row[:4], 0)
    high, low = left_parts(where, row[4:], 1, (high, low))
    total = (384, 768)
    eight = (8, 64, LANES)
    square, near_patterns, away_patterns = product_call(
        square_kernel, "square", where, near[:4] + away[:4] + near[4:] + away[4:], 0, high, low,
        (product_pattern, flag_x), ((392, WIDE_S), eight, eight), (448, WIDE_X),
    )

    near, away = column_blocks(square)
    (begun,) = product_call(
        first_next_kernel, "first_next", where, near, 0, high, low, (near_patterns,), (total,), (392, WIDE_S)
    )
    part = sum_of(near)
    for move in (along(y=2), flip("y")):
        part = part + send(part, move)
    part = after(part, begun)
    for move in (along(xh=1), along(xl=1)):
        part = part + send(part, move)
    (sign_next,) = product_call(
        next_kernel, "next_iterate", where, away, 1, high, low, (away_patterns, begun, product_pattern),
        (total,), (392, WIDE_S), (pltpu.VMEM((BS * 384, LANES), jnp.float32),),
    )
    return lax.cond(
        part[0, LANES] > 0.0,
        lambda: full_rows(sign_iterate, operand_pattern, product_pattern),
        lambda: (sign_next, part[0, 0]),
    )


def flip(axis):
    if axis == "z":
        return lambda a, b, c, d, e: (a, b ^ 1, c, d, e)
    return lambda a, b, c, d, e: (a, b, c, d, e ^ 1)


def solution(mesh):
    spec = P("row", "col")
    return jax.shard_map(
        per_device, mesh=mesh, in_specs=(spec, spec, spec), out_specs=(spec, P()), check_vma=False
    )
```

```python
import functools

import jax
import jax.numpy as jnp
from jax import lax
from jax.experimental import pallas as pl
from jax.experimental.pallas import tpu as pltpu
from jax.sharding import PartitionSpec as P

BS = 6
AXES = ("row", "col")
LANES = 128
SLOTS_X = 42
SLOTS_S = 64
WIDE_X = 256
WIDE_S = 384
VMEM = 26 * 1024 * 1024


def send(value, move):
    pairs = []
    for row in range(16):
        for col in range(8):
            here = (row // 8, row // 2 % 4, row % 2, col // 4, col % 4)
            xh, z, core, xl, y = move(*here)
            pairs.append((row * 8 + col, ((xh % 2) * 8 + (z % 4) * 2 + core % 2) * 8 + (xl % 2) * 4 + y % 4))
    return lax.ppermute(value, AXES, pairs)


def along(xh=0, z=0, core=0, xl=0, y=0):
    return lambda a, b, c, d, e: (a + xh, b + z, c + core, d + xl, e + y)


def dot(a, b):
    return jnp.dot(a, b, preferred_element_type=jnp.float32)


def take(source, index):
    return jnp.take_along_axis(source, index, axis=1, mode="promise_in_bounds")


def lanes_of():
    return lax.broadcasted_iota(jnp.int32, (64, LANES), 1)


def counts(bits):
    before = lax.broadcasted_iota(jnp.int32, (LANES, LANES), 0)
    until = (before <= lax.broadcasted_iota(jnp.int32, (LANES, LANES), 1)).astype(jnp.float32)
    return dot(bits.astype(jnp.bfloat16), until.astype(jnp.bfloat16))


def slot_sources(bits, slots):
    count = counts(bits)
    lane = lanes_of()
    group = sum((lane >= slots * k).astype(jnp.int32) for k in range(1, LANES // slots))
    wanted = (lane - group * slots).astype(jnp.float32)
    position = jnp.zeros(count.shape, jnp.int32)
    for step in (64, 32, 16, 8, 4, 2, 1):
        below = take(count, position + (step - 1)) <= wanted
        position = jnp.where(below, position + step, position)
    return position, group, jnp.max(count[:, LANES - 1 :])


def flag_of(most, slots):
    return jnp.full((8, LANES), jnp.where(most > slots, 1.0, 0.0), jnp.float32)


def pack_kernel(x_ref, pattern_ref, product_ref, left_ref, right_ref, flag_ref, tall_ref):
    for k in range(BS):
        tall_ref[k * 384 : (k + 1) * 384, :] = x_ref[:, k * LANES : (k + 1) * LANES]
    bits = pattern_ref[...].astype(jnp.float32)
    position, group, most = slot_sources(bits, SLOTS_X)
    flag_ref[...] = flag_of(most, SLOTS_X)
    used = lanes_of() < 3 * SLOTS_X
    for t in range(2):
        column = position * BS + (group + 3 * t)
        column = jnp.where(used, column, 0)
        low, high = column & (LANES - 1), column >> 7
        for b in range(BS):
            value = jnp.zeros((64, LANES), jnp.float32)
            for k in range(BS):
                source = tall_ref[pl.ds(k * 384 + b, 64, stride=BS), :]
                value = jnp.where(high == k, take(source, low), value)
            value = jnp.where(used, value, 0.0)
            for out_ref in (left_ref, right_ref):
                out_ref[b * 64 : (b + 1) * 64, t * LANES : (t + 1) * LANES] = value
    product = product_ref[...].astype(jnp.float32)
    for out_ref, first, source in ((left_ref, 384, bits), (right_ref, 384, bits), (right_ref, 416, product)):
        out_ref[first : first + 32, :LANES] = source[:32]
        out_ref[first : first + 32, LANES:] = source[32:]


def split(value):
    high = value.astype(jnp.bfloat16)
    return high, (value - high.astype(jnp.float32)).astype(jnp.bfloat16)


def unpack_steps(packed_ref, bits, slots, put):
    per = LANES // slots
    present = bits > 0.5
    rank = (counts(bits) - bits).astype(jnp.int32)
    spare = per * slots < LANES
    index = jnp.where(present, rank, LANES - 1) if spare else jnp.minimum(rank, slots - 1)

    def one(q, k):
        def run():
            for t in range(BS // per):
                for b in range(BS):
                    parts = []
                    for r in (16 * q, 16 * q + 8):
                        where = index[r : r + 8] + slots * k
                        if spare:
                            where = jnp.minimum(where, LANES - 1)
                        source = packed_ref[b * 64 + r : b * 64 + r + 8, t * LANES : (t + 1) * LANES]
                        value = take(source, where)
                        if not spare:
                            value = jnp.where(present[r : r + 8], value, 0.0)
                        parts.append(value)
                    put(b, t * per + k, 16 * q, *split(jnp.concatenate(parts, axis=0)))

        return run

    return [one(q, k) for q in range(4) for k in range(per)]


def carried(packed_ref, first):
    rows = slice(first, first + 32)
    return jnp.concatenate([packed_ref[rows, :LANES], packed_ref[rows, LANES:]], axis=0)


def fetch(source_ref, target_ref):
    target_ref[...] = source_ref[...]


def left_kernel(where_ref, *refs):
    blocks = refs[:4]
    high_ref, low_ref, stack_ref = refs[-3:]
    step = pl.program_id(0)

    for k in range(4):
        pl.when(step == k)(functools.partial(fetch, blocks[k], stack_ref))

    def put(b, c, r, high, low):
        rows = slice(b * 64 + r, b * 64 + r + 16)
        high_ref[0, rows, c * LANES : (c + 1) * LANES] = high
        low_ref[0, rows, c * LANES : (c + 1) * LANES] = low

    for run in unpack_steps(stack_ref, carried(stack_ref, 384), SLOTS_X, put):
        run()


def unpack_pair(stack_ref, bits, slots, core, high_ref, low_ref):
    steps = []
    for other in range(2):
        first = (core ^ other) * 64

        def put(b, c, r, high, low, first=first):
            rows = pl.ds(pl.multiple_of(first + (b * 128 + r), 16), 16)
            high_ref[rows, c * LANES : (c + 1) * LANES] = high
            low_ref[rows, c * LANES : (c + 1) * LANES] = low

        steps += unpack_steps(stack_ref.at[other], bits[other], slots, put)
    return steps


def multiply(left_high_ref, left_low_ref, high_ref, low_ref, total_ref, others):
    each = len(others) // 3
    for j in range(3):
        for run in others[each * j : each * (j + 1) if j < 2 else None]:
            run()
        span = slice(j * 256, (j + 1) * 256)
        part = dot(left_high_ref[0], high_ref[:, span]) + dot(left_high_ref[0], low_ref[:, span])
        total_ref[:, span] += part + dot(left_low_ref[0], high_ref[:, span])


def product(where_ref, blocks, bits_of, slots, lefts, work, begin, finish):
    stack_a, stack_b, high_a, low_a, high_b, low_b, total_ref = work
    step = pl.program_id(0)
    pairs = len(blocks) // 2
    last = pairs // 2 - 1
    core = where_ref[0] & 1

    def fetch_pair(pair, stack_ref):
        for other in range(2):
            fetch(blocks[pair + pairs * other], stack_ref.at[other])

    def unpack(pair, stack_ref, high_ref, low_ref):
        bits = [bits_of(2 * pair + other, stack_ref.at[other]) for other in range(2)]
        return unpack_pair(stack_ref, bits, slots, core, high_ref, low_ref)

    @pl.when(step == 0)
    def _():
        begin(total_ref)
        fetch_pair(0, stack_a)
        for run in unpack(0, stack_a, high_a, low_a):
            run()

    for k in range(last + 1):
        pl.when(step == k)(functools.partial(fetch_pair, 2 * k + 1, stack_b))

    multiply(*lefts[:2], high_a, low_a, total_ref, unpack(2 * step + 1, stack_b, high_b, low_b))

    for k in range(last):
        pl.when(step == k)(functools.partial(fetch_pair, 2 * k + 2, stack_a))

    @pl.when(step < last)
    def _():
        multiply(*lefts[2:], high_b, low_b, total_ref, unpack(2 * step + 2, stack_a, high_a, low_a))

    @pl.when(step == last)
    def _():
        multiply(*lefts[2:], high_b, low_b, total_ref, [])
        finish(total_ref)


def zero(total_ref):
    total_ref[...] = jnp.zeros_like(total_ref)


def square_kernel(where_ref, *refs):
    blocks, lefts = refs[:16], refs[16:20]
    pattern_ref, flag_x_ref = refs[20:22]
    out_ref, near_ref, away_ref = refs[22:25]

    def finish(total_ref):
        bits = pattern_ref[...].astype(jnp.float32)
        present = bits > 0.5
        position, group, most = slot_sources(bits, SLOTS_S)
        first_rows = where_ref[0] * 64 + lax.broadcasted_iota(jnp.int32, (64, LANES), 0)
        unit = jnp.where(first_rows == where_ref[1] * LANES + lanes_of(), 1.0, 0.0)
        position = jnp.minimum(position, LANES - 1)
        sums = jnp.zeros((64, LANES), jnp.float32)
        for b in range(BS):
            rows = slice(b * 64, (b + 1) * 64)
            for t in range(3):
                values = []
                for c in (2 * t, 2 * t + 1):
                    square = total_ref[rows, c * LANES : (c + 1) * LANES]
                    gap = jnp.where(present, square - unit if b == c else square, 0.0)
                    sums = sums + gap * gap
                    values.append(take(3.0 * unit - square if b == c else -square, position))
                out_ref[rows, t * LANES : (t + 1) * LANES] = jnp.where(group == 0, values[0], values[1])
        flag = jnp.maximum(flag_of(most, SLOTS_S), flag_x_ref[...])
        out_ref[384:392, :LANES] = jnp.full((8, LANES), jnp.sum(sums), jnp.float32)
        out_ref[384:392, LANES : 2 * LANES] = flag
        out_ref[384:392, 2 * LANES :] = flag
        for k, block_ref in enumerate(blocks):
            kept_ref = (near_ref, away_ref)[k // 4 % 2]
            kept_ref[2 * (k % 4) + k // 8] = carried(block_ref, 416)

    bits_of = lambda slot, packed_ref: carried(packed_ref, 384)
    product(where_ref, blocks, bits_of, SLOTS_X, lefts, refs[25:], zero, finish)


def first_next_kernel(where_ref, *refs):
    blocks, lefts = refs[:8], refs[8:12]
    patterns_ref, out_ref = refs[12:14]

    def finish(total_ref):
        out_ref[...] = total_ref[...]

    product(where_ref, blocks, lambda slot, packed_ref: patterns_ref[slot], SLOTS_S, lefts, refs[14:], zero, finish)


def next_kernel(where_ref, *refs):
    blocks, lefts = refs[:8], refs[8:12]
    patterns_ref, before_ref, pattern_ref = refs[12:15]
    out_ref, tall_ref = refs[15:17]

    def begin(total_ref):
        total_ref[...] = before_ref[...]

    def finish(total_ref):
        present = pattern_ref[...] > 0
        for j in range(BS):
            lane = lanes_of() + j * LANES
            molecule = (lane * 10923) >> 16
            function = lane - molecule * BS
            for b in range(BS):
                value = jnp.zeros((64, LANES), jnp.float32)
                for c in range(BS):
                    source = total_ref[b * 64 : (b + 1) * 64, c * LANES : (c + 1) * LANES]
                    source = jnp.where(present, 0.5 * source, 0.0)
                    value = jnp.where(function == c, take(source, molecule), value)
                tall_ref[pl.ds(j * 384 + b, 64, stride=BS), :] = value
            out_ref[:, j * LANES : (j + 1) * LANES] = tall_ref[j * 384 : (j + 1) * 384, :]

    product(where_ref, blocks, lambda slot, packed_ref: patterns_ref[slot], SLOTS_S, lefts, refs[17:], begin, finish)


ANY = pl.BlockSpec(memory_space=pl.ANY)
HELD = pl.BlockSpec(memory_space=pltpu.VMEM)


def whole(shape):
    return pl.BlockSpec(shape, lambda i, where: (0,) * len(shape))


def params():
    return pltpu.CompilerParams(vmem_limit_bytes=VMEM)


def f32(*shape):
    return jax.ShapeDtypeStruct(shape, jnp.float32)


def cost(us):
    return pl.CostEstimate(flops=int(us * 1_000_000_000), bytes_accessed=int(us * 500_000), transcendentals=0)


def pack(x, operand, product):
    return pl.pallas_call(
        pack_kernel,
        out_shape=(f32(416, WIDE_X), f32(448, WIDE_X), f32(8, LANES)),
        scratch_shapes=[pltpu.VMEM((BS * 384, LANES), jnp.float32)],
        compiler_params=params(),
        name="pack",
    )(x, operand, product)


def left_parts(where, blocks, second, earlier=()):
    part = pl.BlockSpec((1, 384, 768), lambda i, where: (row_place(where, i + 4 * second), 0, 0))
    return pl.pallas_call(
        left_kernel,
        grid_spec=pltpu.PrefetchScalarGridSpec(
            num_scalar_prefetch=1,
            grid=(4,),
            in_specs=[HELD] * 4 + [ANY] * len(earlier),
            out_specs=[part, part],
            scratch_shapes=[pltpu.VMEM((416, WIDE_X), jnp.float32)],
        ),
        out_shape=[jax.ShapeDtypeStruct((8, 384, 768), jnp.bfloat16)] * 2,
        input_output_aliases={5 + k: k for k in range(len(earlier))},
        compiler_params=params(),
        cost_estimate=cost(5),
        name="left_parts",
    )(where, *blocks, *earlier)


def product_call(kernel, name, where, blocks, second, high, low, rest, outs, stack, scratch=()):
    pairs = len(blocks) // 2
    even = pl.BlockSpec((1, 384, 768), lambda i, where: (column_pair(where, second + i // 2, i % 2), 0, 0))
    odd = pl.BlockSpec((1, 384, 768), lambda i, where: (column_pair(where, second + i // 2, 3 - i % 2), 0, 0))
    return pl.pallas_call(
        kernel,
        grid_spec=pltpu.PrefetchScalarGridSpec(
            num_scalar_prefetch=1,
            grid=(pairs // 2,),
            in_specs=[HELD] * len(blocks) + [even, even, odd, odd] + [whole(t.shape) for t in rest],
            out_specs=[whole(shape) for shape in outs],
            scratch_shapes=[*scratch]
            + [pltpu.VMEM((2, *stack), jnp.float32)] * 2
            + [pltpu.VMEM((768, 768), jnp.bfloat16)] * 4
            + [pltpu.VMEM((384, 768), jnp.float32)],
        ),
        out_shape=[f32(*shape) for shape in outs],
        compiler_params=params(),
        cost_estimate=cost(2.5 * pairs),
        name=name,
    )(where, *blocks, high, low, high, low, *rest)


def after(value, *earlier):
    return lax.optimization_barrier((value, *earlier))[0]


GATES = {"U": ("H",), "u": ("l",), "D": ("F",), "d": ("f",)}
GATES_S = {"C": ("U",), "CH": ("F",)}


def run_moves(table, gates, done):
    def get(name):
        if name not in done:
            source, move = table[name]
            value = get(source)
            if name in gates:
                value = after(value, *(get(g) for g in gates[name]))
            done[name] = send(value, move)
        return done[name]

    for name in table:
        get(name)
    return done


def both_blocks(left, right):
    table = dict([
        ("H", ("R", along(xh=1))),
        ("l", ("L", along(xl=1))),
        ("U", ("R", along(z=1))),
        ("u", ("L", along(y=1))),
        ("D", ("R", along(z=-1))),
        ("d", ("L", along(y=-1))),
        ("F", ("R", along(z=2))),
        ("f", ("L", along(y=2))),
        ("C", ("R", along(core=1))),
        ("HU", ("H", along(z=1))),
        ("lu", ("l", along(y=1))),
        ("HD", ("H", along(z=-1))),
        ("ld", ("l", along(y=-1))),
        ("HF", ("F", along(xh=1))),
        ("lf", ("f", along(xl=1))),
        ("CU", ("U", along(core=1))),
        ("CD", ("D", along(core=1))),
        ("CF", ("F", along(core=1))),
        ("CH", ("H", along(core=1))),
        ("CHU", ("HU", along(core=1))),
        ("CHD", ("HD", along(core=1))),
        ("CHF", ("HF", along(core=1))),
    ])
    done = run_moves(table, GATES, {"R": right, "L": left})
    near = [done[k] for k in ("R", "U", "D", "F", "C", "CU", "CD", "CF")]
    away = [done[k] for k in ("H", "HU", "HD", "HF", "CH", "CHU", "CHD", "CHF")]
    row = [done[k] for k in ("L", "u", "d", "f", "l", "lu", "ld", "lf")]
    return row, near, away


def column_blocks(own):
    table = dict([
        ("U", ("R", along(z=1))),
        ("D", ("R", along(z=-1))),
        ("H", ("R", along(xh=1))),
        ("F", ("R", along(z=2))),
        ("C", ("R", along(core=1))),
        ("HU", ("H", along(z=1))),
        ("HD", ("H", along(z=-1))),
        ("CU", ("U", along(core=1))),
        ("CD", ("D", along(core=1))),
        ("CH", ("H", along(core=1))),
        ("HF", ("F", along(xh=1))),
        ("CF", ("F", along(core=1))),
        ("CHU", ("HU", along(core=1))),
        ("CHD", ("HD", along(core=1))),
        ("CHF", ("HF", along(core=1))),
    ])
    done = run_moves(table, GATES_S, {"R": own})
    near = [done[k] for k in ("R", "U", "D", "F", "C", "CU", "CD", "CF")]
    away = [done[k] for k in ("H", "HU", "HD", "HF", "CH", "CHU", "CHD", "CHF")]
    return near, away


def column_pair(where, second, b):
    row = where[0]
    return ((row >> 3) ^ second) * 4 + (((row >> 1) + b) & 3)


def row_place(where_ref, k):
    col = where_ref[1]
    place = k & 3
    b = jnp.where(place == 0, 0, jnp.where(place == 1, 3, place - 1))
    return ((col >> 2) ^ (k >> 2)) * 4 + ((col + b) & 3)


def expand_blocks(pattern):
    rows, cols = pattern.shape
    wide = jnp.broadcast_to(pattern.astype(jnp.float32)[:, None, :, None], (rows, BS, cols, BS))
    return wide.reshape(rows * BS, cols * BS)


def matmul_high(left, right):
    return jnp.dot(left, right, precision=lax.Precision.HIGHEST, preferred_element_type=jnp.float32)


def gathered(value, name, axis):
    count = lax.axis_size(name)
    here = lax.axis_index(name)
    ring = [(i, (i + 1) % count) for i in range(count)]

    def body(k, state):
        value, kept = state
        kept = lax.dynamic_update_slice_in_dim(kept, value, (here - k + count) % count * value.shape[axis], axis)
        return lax.ppermute(value, name, ring), kept

    shape = [n * count if d == axis else n for d, n in enumerate(value.shape)]
    return lax.fori_loop(0, count, body, (value, jnp.zeros(shape, value.dtype)))[1]


def full_rows(sign_iterate, operand_pattern, product_pattern):
    local_rows, local_cols = sign_iterate.shape
    product_mask = expand_blocks(product_pattern)
    sparse_iterate = sign_iterate * expand_blocks(operand_pattern)
    entry_rows = lax.axis_index("row") * local_rows + jnp.arange(local_rows, dtype=jnp.int32)
    entry_cols = lax.axis_index("col") * local_cols + jnp.arange(local_cols, dtype=jnp.int32)
    identity = (entry_rows[:, None] == entry_cols[None, :]).astype(jnp.float32)
    left = gathered(sparse_iterate, "col", 1)
    square = matmul_high(left, gathered(sparse_iterate, "row", 0)) * product_mask
    polynomial = 3.0 * identity - square
    sign_next = 0.5 * matmul_high(left, gathered(polynomial, "row", 0)) * product_mask
    defect = jnp.sum((square - identity) ** 2).reshape(1, 1)
    for move in (along(core=1), along(xh=1), along(z=2), flip("z"), along(xl=1), along(y=2), flip("y")):
        defect = defect + send(defect, move)
    return sign_next, defect[0, 0]


def sum_of(blocks):
    own, up, down, far = (a[384:385, :256] + b[384:385, :256] for a, b in zip(blocks[:4], blocks[4:]))
    return (own + far) + (up + down)


def per_device(sign_iterate, operand_pattern, product_pattern):
    left, right, flag_x = pack(sign_iterate, operand_pattern, product_pattern)
    where = jnp.stack([lax.axis_index("row"), lax.axis_index("col")]).astype(jnp.int32)
    row, near, away = both_blocks(left, right)
    high, low = left_parts(where, row[:4], 0)
    high, low = left_parts(where, row[4:], 1, (high, low))
    total = (384, 768)
    eight = (8, 64, LANES)
    square, near_patterns, away_patterns = product_call(
        square_kernel, "square", where, near[:4] + away[:4] + near[4:] + away[4:], 0, high, low,
        (product_pattern, flag_x), ((392, WIDE_S), eight, eight), (448, WIDE_X),
    )

    near, away = column_blocks(square)
    (begun,) = product_call(
        first_next_kernel, "first_next", where, near, 0, high, low, (near_patterns,), (total,), (392, WIDE_S)
    )
    part = sum_of(near)
    for move in (along(y=2), flip("y"), along(xh=1), along(xl=1)):
        part = part + send(part, move)
    (sign_next,) = product_call(
        next_kernel, "next_iterate", where, away, 1, high, low, (away_patterns, begun, product_pattern),
        (total,), (392, WIDE_S), (pltpu.VMEM((BS * 384, LANES), jnp.float32),),
    )
    return lax.cond(
        part[0, LANES] > 0.0,
        lambda: full_rows(sign_iterate, operand_pattern, product_pattern),
        lambda: (sign_next, part[0, 0]),
    )


def flip(axis):
    if axis == "z":
        return lambda a, b, c, d, e: (a, b ^ 1, c, d, e)
    return lambda a, b, c, d, e: (a, b, c, d, e ^ 1)


def solution(mesh):
    spec = P("row", "col")
    return jax.shard_map(
        per_device, mesh=mesh, in_specs=(spec, spec, spec), out_specs=(spec, P()), check_vma=False
    )
```

```python
import functools

import jax
import jax.numpy as jnp
from jax import lax
from jax.experimental import pallas as pl
from jax.experimental.pallas import tpu as pltpu
from jax.sharding import PartitionSpec as P

BS = 6
AXES = ("row", "col")
LANES = 128
SLOTS_X = 42
SLOTS_S = 64
WIDE_X = 256
WIDE_S = 384
VMEM = 26 * 1024 * 1024


def send(value, move):
    pairs = []
    for row in range(16):
        for col in range(8):
            here = (row // 8, row // 2 % 4, row % 2, col // 4, col % 4)
            xh, z, core, xl, y = move(*here)
            pairs.append((row * 8 + col, ((xh % 2) * 8 + (z % 4) * 2 + core % 2) * 8 + (xl % 2) * 4 + y % 4))
    return lax.ppermute(value, AXES, pairs)


def along(xh=0, z=0, core=0, xl=0, y=0):
    return lambda a, b, c, d, e: (a + xh, b + z, c + core, d + xl, e + y)


def dot(a, b):
    return jnp.dot(a, b, preferred_element_type=jnp.float32)


def take(source, index):
    return jnp.take_along_axis(source, index, axis=1, mode="promise_in_bounds")


def lanes_of():
    return lax.broadcasted_iota(jnp.int32, (64, LANES), 1)


def counts(bits):
    before = lax.broadcasted_iota(jnp.int32, (LANES, LANES), 0)
    until = (before <= lax.broadcasted_iota(jnp.int32, (LANES, LANES), 1)).astype(jnp.float32)
    return dot(bits.astype(jnp.bfloat16), until.astype(jnp.bfloat16))


def slot_sources(bits, slots):
    count = counts(bits)
    lane = lanes_of()
    group = sum((lane >= slots * k).astype(jnp.int32) for k in range(1, LANES // slots))
    wanted = (lane - group * slots).astype(jnp.float32)
    position = jnp.zeros(count.shape, jnp.int32)
    for step in (64, 32, 16, 8, 4, 2, 1):
        below = take(count, position + (step - 1)) <= wanted
        position = jnp.where(below, position + step, position)
    return position, group, jnp.max(count[:, LANES - 1 :])


def flag_of(most, slots):
    return jnp.full((8, LANES), jnp.where(most > slots, 1.0, 0.0), jnp.float32)


def pack_kernel(x_ref, pattern_ref, product_ref, left_ref, right_ref, flag_ref, tall_ref):
    for k in range(BS):
        tall_ref[k * 384 : (k + 1) * 384, :] = x_ref[:, k * LANES : (k + 1) * LANES]
    bits = pattern_ref[...].astype(jnp.float32)
    position, group, most = slot_sources(bits, SLOTS_X)
    flag_ref[...] = flag_of(most, SLOTS_X)
    used = lax.broadcasted_iota(jnp.int32, (8, LANES), 1) < 3 * SLOTS_X
    for r in range(0, 64, 8):
        for t in range(2):
            column = position[r : r + 8] * BS + (group[r : r + 8] + 3 * t)
            column = jnp.where(used, column, 0)
            low, high = column & (LANES - 1), column >> 7
            for b in range(BS):
                value = jnp.zeros((8, LANES), jnp.float32)
                for k in range(BS):
                    source = tall_ref[pl.ds(k * 384 + r * BS + b, 8, stride=BS), :]
                    value = jnp.where(high == k, take(source, low), value)
                value = jnp.where(used, value, 0.0)
                for out_ref in (left_ref, right_ref):
                    out_ref[b * 64 + r : b * 64 + r + 8, t * LANES : (t + 1) * LANES] = value
    product = product_ref[...].astype(jnp.float32)
    for out_ref, first, source in ((left_ref, 384, bits), (right_ref, 384, bits), (right_ref, 416, product)):
        out_ref[first : first + 32, :LANES] = source[:32]
        out_ref[first : first + 32, LANES:] = source[32:]


def split(value):
    high = value.astype(jnp.bfloat16)
    return high, (value - high.astype(jnp.float32)).astype(jnp.bfloat16)


def unpack_steps(packed_ref, bits, slots, put):
    per = LANES // slots
    present = bits > 0.5
    rank = (counts(bits) - bits).astype(jnp.int32)
    spare = per * slots < LANES
    index = jnp.where(present, rank, LANES - 1) if spare else jnp.minimum(rank, slots - 1)

    def one(q, k):
        def run():
            for t in range(BS // per):
                for b in range(BS):
                    parts = []
                    for r in (16 * q, 16 * q + 8):
                        where = index[r : r + 8] + slots * k
                        if spare:
                            where = jnp.minimum(where, LANES - 1)
                        source = packed_ref[b * 64 + r : b * 64 + r + 8, t * LANES : (t + 1) * LANES]
                        value = take(source, where)
                        if not spare:
                            value = jnp.where(present[r : r + 8], value, 0.0)
                        parts.append(value)
                    put(b, t * per + k, 16 * q, *split(jnp.concatenate(parts, axis=0)))

        return run

    return [one(q, k) for q in range(4) for k in range(per)]


def carried(packed_ref, first):
    rows = slice(first, first + 32)
    return jnp.concatenate([packed_ref[rows, :LANES], packed_ref[rows, LANES:]], axis=0)


def fetch(source_ref, target_ref):
    target_ref[...] = source_ref[...]


def left_kernel(where_ref, *refs):
    blocks = refs[:4]
    high_ref, low_ref, stack_ref = refs[-3:]
    step = pl.program_id(0)

    for k in range(4):
        pl.when(step == k)(functools.partial(fetch, blocks[k], stack_ref))

    def put(b, c, r, high, low):
        rows = slice(b * 64 + r, b * 64 + r + 16)
        high_ref[0, rows, c * LANES : (c + 1) * LANES] = high
        low_ref[0, rows, c * LANES : (c + 1) * LANES] = low

    for run in unpack_steps(stack_ref, carried(stack_ref, 384), SLOTS_X, put):
        run()


def unpack_pair(stack_ref, bits, slots, core, high_ref, low_ref):
    steps = []
    for other in range(2):
        first = (core ^ other) * 64

        def put(b, c, r, high, low, first=first):
            rows = pl.ds(pl.multiple_of(first + (b * 128 + r), 16), 16)
            high_ref[rows, c * LANES : (c + 1) * LANES] = high
            low_ref[rows, c * LANES : (c + 1) * LANES] = low

        steps += unpack_steps(stack_ref.at[other], bits[other], slots, put)
    return steps


def multiply(left_high_ref, left_low_ref, high_ref, low_ref, total_ref, others):
    each = len(others) // 3
    for j in range(3):
        for run in others[each * j : each * (j + 1) if j < 2 else None]:
            run()
        span = slice(j * 256, (j + 1) * 256)
        part = dot(left_high_ref[0], high_ref[:, span]) + dot(left_high_ref[0], low_ref[:, span])
        total_ref[:, span] += part + dot(left_low_ref[0], high_ref[:, span])


def product(where_ref, blocks, bits_of, slots, lefts, work, begin, finish):
    stack_a, stack_b, high_a, low_a, high_b, low_b, total_ref = work
    step = pl.program_id(0)
    pairs = len(blocks) // 2
    last = pairs // 2 - 1
    core = where_ref[0] & 1

    def fetch_pair(pair, stack_ref):
        for other in range(2):
            fetch(blocks[pair + pairs * other], stack_ref.at[other])

    def unpack(pair, stack_ref, high_ref, low_ref):
        bits = [bits_of(2 * pair + other, stack_ref.at[other]) for other in range(2)]
        return unpack_pair(stack_ref, bits, slots, core, high_ref, low_ref)

    @pl.when(step == 0)
    def _():
        begin(total_ref)
        fetch_pair(0, stack_a)
        for run in unpack(0, stack_a, high_a, low_a):
            run()

    for k in range(last + 1):
        pl.when(step == k)(functools.partial(fetch_pair, 2 * k + 1, stack_b))

    multiply(*lefts[:2], high_a, low_a, total_ref, unpack(2 * step + 1, stack_b, high_b, low_b))

    for k in range(last):
        pl.when(step == k)(functools.partial(fetch_pair, 2 * k + 2, stack_a))

    @pl.when(step < last)
    def _():
        multiply(*lefts[2:], high_b, low_b, total_ref, unpack(2 * step + 2, stack_a, high_a, low_a))

    @pl.when(step == last)
    def _():
        multiply(*lefts[2:], high_b, low_b, total_ref, [])
        finish(total_ref)


def zero(total_ref):
    total_ref[...] = jnp.zeros_like(total_ref)


def square_kernel(where_ref, *refs):
    blocks, lefts = refs[:16], refs[16:20]
    pattern_ref, flag_x_ref = refs[20:22]
    out_ref, near_ref, away_ref = refs[22:25]

    def finish(total_ref):
        bits = pattern_ref[...].astype(jnp.float32)
        present = bits > 0.5
        position, group, most = slot_sources(bits, SLOTS_S)
        first_rows = where_ref[0] * 64 + lax.broadcasted_iota(jnp.int32, (64, LANES), 0)
        unit = jnp.where(first_rows == where_ref[1] * LANES + lanes_of(), 1.0, 0.0)
        position = jnp.minimum(position, LANES - 1)
        sums = jnp.zeros((8, LANES), jnp.float32)
        for r in range(0, 64, 8):
            here, kept, eye, second = position[r : r + 8], present[r : r + 8], unit[r : r + 8], group[r : r + 8] > 0
            for b in range(BS):
                rows = slice(b * 64 + r, b * 64 + r + 8)
                for t in range(3):
                    values = []
                    for c in (2 * t, 2 * t + 1):
                        square = total_ref[rows, c * LANES : (c + 1) * LANES]
                        gap = jnp.where(kept, square - eye if b == c else square, 0.0)
                        sums = sums + gap * gap
                        values.append(take(3.0 * eye - square if b == c else -square, here))
                    out_ref[rows, t * LANES : (t + 1) * LANES] = jnp.where(second, values[1], values[0])
        flag = jnp.maximum(flag_of(most, SLOTS_S), flag_x_ref[...])
        out_ref[384:392, :LANES] = jnp.full((8, LANES), jnp.sum(sums), jnp.float32)
        out_ref[384:392, LANES : 2 * LANES] = flag
        out_ref[384:392, 2 * LANES :] = flag
        for k, block_ref in enumerate(blocks):
            kept_ref = (near_ref, away_ref)[k // 4 % 2]
            kept_ref[2 * (k % 4) + k // 8] = carried(block_ref, 416)

    bits_of = lambda slot, packed_ref: carried(packed_ref, 384)
    product(where_ref, blocks, bits_of, SLOTS_X, lefts, refs[25:], zero, finish)


def first_next_kernel(where_ref, *refs):
    blocks, lefts = refs[:8], refs[8:12]
    patterns_ref, out_ref = refs[12:14]

    def finish(total_ref):
        out_ref[...] = total_ref[...]

    product(where_ref, blocks, lambda slot, packed_ref: patterns_ref[slot], SLOTS_S, lefts, refs[14:], zero, finish)


def next_kernel(where_ref, *refs):
    blocks, lefts = refs[:8], refs[8:12]
    patterns_ref, before_ref, pattern_ref = refs[12:15]
    out_ref, tall_ref = refs[15:17]

    def begin(total_ref):
        total_ref[...] = before_ref[...]

    def finish(total_ref):
        present = pattern_ref[...] > 0
        for b in range(BS):
            rows = slice(b * 64, (b + 1) * 64)
            for c in range(BS):
                span = slice(c * LANES, (c + 1) * LANES)
                total_ref[rows, span] = jnp.where(present, 0.5 * total_ref[rows, span], 0.0)
        for j in range(BS):
            lane = lanes_of() + j * LANES
            molecule = (lane * 10923) >> 16
            function = lane - molecule * BS
            for b in range(BS):
                value = jnp.zeros((64, LANES), jnp.float32)
                for c in range(BS):
                    source = total_ref[b * 64 : (b + 1) * 64, c * LANES : (c + 1) * LANES]
                    value = jnp.where(function == c, take(source, molecule), value)
                tall_ref[pl.ds(j * 384 + b, 64, stride=BS), :] = value
            out_ref[:, j * LANES : (j + 1) * LANES] = tall_ref[j * 384 : (j + 1) * 384, :]

    product(where_ref, blocks, lambda slot, packed_ref: patterns_ref[slot], SLOTS_S, lefts, refs[17:], begin, finish)


ANY = pl.BlockSpec(memory_space=pl.ANY)
HELD = pl.BlockSpec(memory_space=pltpu.VMEM)


def whole(shape):
    return pl.BlockSpec(shape, lambda i, where: (0,) * len(shape))


def params():
    return pltpu.CompilerParams(vmem_limit_bytes=VMEM)


def f32(*shape):
    return jax.ShapeDtypeStruct(shape, jnp.float32)


def cost(us):
    return pl.CostEstimate(flops=int(us * 1_000_000_000), bytes_accessed=int(us * 500_000), transcendentals=0)


def pack(x, operand, product):
    return pl.pallas_call(
        pack_kernel,
        out_shape=(f32(416, WIDE_X), f32(448, WIDE_X), f32(8, LANES)),
        scratch_shapes=[pltpu.VMEM((BS * 384, LANES), jnp.float32)],
        compiler_params=params(),
        name="pack",
    )(x, operand, product)


def left_parts(where, blocks, second, earlier=()):
    part = pl.BlockSpec((1, 384, 768), lambda i, where: (row_place(where, i + 4 * second), 0, 0))
    return pl.pallas_call(
        left_kernel,
        grid_spec=pltpu.PrefetchScalarGridSpec(
            num_scalar_prefetch=1,
            grid=(4,),
            in_specs=[HELD] * 4 + [ANY] * len(earlier),
            out_specs=[part, part],
            scratch_shapes=[pltpu.VMEM((416, WIDE_X), jnp.float32)],
        ),
        out_shape=[jax.ShapeDtypeStruct((8, 384, 768), jnp.bfloat16)] * 2,
        input_output_aliases={5 + k: k for k in range(len(earlier))},
        compiler_params=params(),
        cost_estimate=cost(5),
        name="left_parts",
    )(where, *blocks, *earlier)


def product_call(kernel, name, where, blocks, second, high, low, rest, outs, stack, scratch=()):
    pairs = len(blocks) // 2
    even = pl.BlockSpec((1, 384, 768), lambda i, where: (column_pair(where, second + i // 2, i % 2), 0, 0))
    odd = pl.BlockSpec((1, 384, 768), lambda i, where: (column_pair(where, second + i // 2, 3 - i % 2), 0, 0))
    return pl.pallas_call(
        kernel,
        grid_spec=pltpu.PrefetchScalarGridSpec(
            num_scalar_prefetch=1,
            grid=(pairs // 2,),
            in_specs=[HELD] * len(blocks) + [even, even, odd, odd] + [whole(t.shape) for t in rest],
            out_specs=[whole(shape) for shape in outs],
            scratch_shapes=[*scratch]
            + [pltpu.VMEM((2, *stack), jnp.float32)] * 2
            + [pltpu.VMEM((768, 768), jnp.bfloat16)] * 4
            + [pltpu.VMEM((384, 768), jnp.float32)],
        ),
        out_shape=[f32(*shape) for shape in outs],
        compiler_params=params(),
        cost_estimate=cost(2.5 * pairs),
        name=name,
    )(where, *blocks, high, low, high, low, *rest)


def after(value, *earlier):
    return lax.optimization_barrier((value, *earlier))[0]


GATES = {"U": ("H",), "u": ("l",), "D": ("F",), "d": ("f",)}
GATES_S = {"C": ("U",), "CH": ("F",)}


def run_moves(table, gates, done):
    def get(name):
        if name not in done:
            source, move = table[name]
            value = get(source)
            if name in gates:
                value = after(value, *(get(g) for g in gates[name]))
            done[name] = send(value, move)
        return done[name]

    for name in table:
        get(name)
    return done


def both_blocks(left, right):
    table = dict([
        ("H", ("R", along(xh=1))),
        ("l", ("L", along(xl=1))),
        ("U", ("R", along(z=1))),
        ("u", ("L", along(y=1))),
        ("D", ("R", along(z=-1))),
        ("d", ("L", along(y=-1))),
        ("F", ("R", along(z=2))),
        ("f", ("L", along(y=2))),
        ("C", ("R", along(core=1))),
        ("HU", ("H", along(z=1))),
        ("lu", ("l", along(y=1))),
        ("HD", ("H", along(z=-1))),
        ("ld", ("l", along(y=-1))),
        ("HF", ("F", along(xh=1))),
        ("lf", ("f", along(xl=1))),
        ("CU", ("U", along(core=1))),
        ("CD", ("D", along(core=1))),
        ("CF", ("F", along(core=1))),
        ("CH", ("H", along(core=1))),
        ("CHU", ("HU", along(core=1))),
        ("CHD", ("HD", along(core=1))),
        ("CHF", ("HF", along(core=1))),
    ])
    done = run_moves(table, GATES, {"R": right, "L": left})
    near = [done[k] for k in ("R", "U", "D", "F", "C", "CU", "CD", "CF")]
    away = [done[k] for k in ("H", "HU", "HD", "HF", "CH", "CHU", "CHD", "CHF")]
    row = [done[k] for k in ("L", "u", "d", "f", "l", "lu", "ld", "lf")]
    return row, near, away


def column_blocks(own):
    table = dict([
        ("U", ("R", along(z=1))),
        ("D", ("R", along(z=-1))),
        ("H", ("R", along(xh=1))),
        ("F", ("R", along(z=2))),
        ("C", ("R", along(core=1))),
        ("HU", ("H", along(z=1))),
        ("HD", ("H", along(z=-1))),
        ("CU", ("U", along(core=1))),
        ("CD", ("D", along(core=1))),
        ("CH", ("H", along(core=1))),
        ("HF", ("F", along(xh=1))),
        ("CF", ("F", along(core=1))),
        ("CHU", ("HU", along(core=1))),
        ("CHD", ("HD", along(core=1))),
        ("CHF", ("HF", along(core=1))),
    ])
    done = run_moves(table, GATES_S, {"R": own})
    near = [done[k] for k in ("R", "U", "D", "F", "C", "CU", "CD", "CF")]
    away = [done[k] for k in ("H", "HU", "HD", "HF", "CH", "CHU", "CHD", "CHF")]
    return near, away


def column_pair(where, second, b):
    row = where[0]
    return ((row >> 3) ^ second) * 4 + (((row >> 1) + b) & 3)


def row_place(where_ref, k):
    col = where_ref[1]
    place = k & 3
    b = jnp.where(place == 0, 0, jnp.where(place == 1, 3, place - 1))
    return ((col >> 2) ^ (k >> 2)) * 4 + ((col + b) & 3)


def expand_blocks(pattern):
    rows, cols = pattern.shape
    wide = jnp.broadcast_to(pattern.astype(jnp.float32)[:, None, :, None], (rows, BS, cols, BS))
    return wide.reshape(rows * BS, cols * BS)


def matmul_high(left, right):
    return jnp.dot(left, right, precision=lax.Precision.HIGHEST, preferred_element_type=jnp.float32)


def gathered(value, name, axis):
    count = lax.axis_size(name)
    here = lax.axis_index(name)
    ring = [(i, (i + 1) % count) for i in range(count)]

    def body(k, state):
        value, kept = state
        kept = lax.dynamic_update_slice_in_dim(kept, value, (here - k + count) % count * value.shape[axis], axis)
        return lax.ppermute(value, name, ring), kept

    shape = [n * count if d == axis else n for d, n in enumerate(value.shape)]
    return lax.fori_loop(0, count, body, (value, jnp.zeros(shape, value.dtype)))[1]


def full_rows(sign_iterate, operand_pattern, product_pattern):
    local_rows, local_cols = sign_iterate.shape
    product_mask = expand_blocks(product_pattern)
    sparse_iterate = sign_iterate * expand_blocks(operand_pattern)
    entry_rows = lax.axis_index("row") * local_rows + jnp.arange(local_rows, dtype=jnp.int32)
    entry_cols = lax.axis_index("col") * local_cols + jnp.arange(local_cols, dtype=jnp.int32)
    identity = (entry_rows[:, None] == entry_cols[None, :]).astype(jnp.float32)
    left = gathered(sparse_iterate, "col", 1)
    square = matmul_high(left, gathered(sparse_iterate, "row", 0)) * product_mask
    polynomial = 3.0 * identity - square
    sign_next = 0.5 * matmul_high(left, gathered(polynomial, "row", 0)) * product_mask
    defect = jnp.sum((square - identity) ** 2).reshape(1, 1)
    for move in (along(core=1), along(xh=1), along(z=2), flip("z"), along(xl=1), along(y=2), flip("y")):
        defect = defect + send(defect, move)
    return sign_next, defect[0, 0]


def sum_of(blocks):
    own, up, down, far = (a[384:385, :256] + b[384:385, :256] for a, b in zip(blocks[:4], blocks[4:]))
    return (own + far) + (up + down)


def per_device(sign_iterate, operand_pattern, product_pattern):
    left, right, flag_x = pack(sign_iterate, operand_pattern, product_pattern)
    where = jnp.stack([lax.axis_index("row"), lax.axis_index("col")]).astype(jnp.int32)
    row, near, away = both_blocks(left, right)
    high, low = left_parts(where, row[:4], 0)
    high, low = left_parts(where, row[4:], 1, (high, low))
    total = (384, 768)
    eight = (8, 64, LANES)
    square, near_patterns, away_patterns = product_call(
        square_kernel, "square", where, near[:4] + away[:4] + near[4:] + away[4:], 0, high, low,
        (product_pattern, flag_x), ((392, WIDE_S), eight, eight), (448, WIDE_X),
    )

    near, away = column_blocks(square)
    (begun,) = product_call(
        first_next_kernel, "first_next", where, near, 0, high, low, (near_patterns,), (total,), (392, WIDE_S)
    )
    part = sum_of(near)
    for move in (along(y=2), flip("y"), along(xh=1), along(xl=1)):
        part = part + send(part, move)
    (sign_next,) = product_call(
        next_kernel, "next_iterate", where, away, 1, high, low, (away_patterns, begun, product_pattern),
        (total,), (392, WIDE_S), (pltpu.VMEM((BS * 384, LANES), jnp.float32),),
    )
    return lax.cond(
        part[0, LANES] > 0.0,
        lambda: full_rows(sign_iterate, operand_pattern, product_pattern),
        lambda: (sign_next, part[0, 0]),
    )


def flip(axis):
    if axis == "z":
        return lambda a, b, c, d, e: (a, b ^ 1, c, d, e)
    return lambda a, b, c, d, e: (a, b, c, d, e ^ 1)


def solution(mesh):
    spec = P("row", "col")
    return jax.shard_map(
        per_device, mesh=mesh, in_specs=(spec, spec, spec), out_specs=(spec, P()), check_vma=False
    )
```

```python
import functools

import jax
import jax.numpy as jnp
from jax import lax
from jax.experimental import pallas as pl
from jax.experimental.pallas import tpu as pltpu
from jax.sharding import PartitionSpec as P

BS = 6
AXES = ("row", "col")
LANES = 128
SLOTS_X = 42
SLOTS_S = 64
WIDE_X = 256
WIDE_S = 384
VMEM = 26 * 1024 * 1024


def send(value, move):
    pairs = []
    for row in range(16):
        for col in range(8):
            here = (row // 8, row // 2 % 4, row % 2, col // 4, col % 4)
            xh, z, core, xl, y = move(*here)
            pairs.append((row * 8 + col, ((xh % 2) * 8 + (z % 4) * 2 + core % 2) * 8 + (xl % 2) * 4 + y % 4))
    return lax.ppermute(value, AXES, pairs)


def along(xh=0, z=0, core=0, xl=0, y=0):
    return lambda a, b, c, d, e: (a + xh, b + z, c + core, d + xl, e + y)


def dot(a, b):
    return jnp.dot(a, b, preferred_element_type=jnp.float32)


def take(source, index):
    return jnp.take_along_axis(source, index, axis=1, mode="promise_in_bounds")


def lanes_of():
    return lax.broadcasted_iota(jnp.int32, (64, LANES), 1)


def counts(bits):
    before = lax.broadcasted_iota(jnp.int32, (LANES, LANES), 0)
    until = (before <= lax.broadcasted_iota(jnp.int32, (LANES, LANES), 1)).astype(jnp.float32)
    return dot(bits.astype(jnp.bfloat16), until.astype(jnp.bfloat16))


def slot_sources(bits, slots):
    count = counts(bits)
    lane = lanes_of()
    group = sum((lane >= slots * k).astype(jnp.int32) for k in range(1, LANES // slots))
    wanted = (lane - group * slots).astype(jnp.float32)
    position = jnp.zeros(count.shape, jnp.int32)
    for step in (64, 32, 16, 8, 4, 2, 1):
        below = take(count, position + (step - 1)) <= wanted
        position = jnp.where(below, position + step, position)
    return position, group, jnp.max(count[:, LANES - 1 :])


def flag_of(most, slots):
    return jnp.full((8, LANES), jnp.where(most > slots, 1.0, 0.0), jnp.float32)


def pack_kernel(x_ref, pattern_ref, product_ref, left_ref, right_ref, flag_ref, tall_ref):
    for k in range(BS):
        tall_ref[k * 384 : (k + 1) * 384, :] = x_ref[:, k * LANES : (k + 1) * LANES]
    bits = pattern_ref[...].astype(jnp.float32)
    position, group, most = slot_sources(bits, SLOTS_X)
    flag_ref[...] = flag_of(most, SLOTS_X)
    used = lax.broadcasted_iota(jnp.int32, (8, LANES), 1) < 3 * SLOTS_X
    for r in range(0, 64, 8):
        for t in range(2):
            column = position[r : r + 8] * BS + (group[r : r + 8] + 3 * t)
            column = jnp.where(used, column, 0)
            low, high = column & (LANES - 1), column >> 7
            for b in range(BS):
                value = jnp.zeros((8, LANES), jnp.float32)
                for k in range(BS):
                    source = tall_ref[pl.ds(k * 384 + r * BS + b, 8, stride=BS), :]
                    value = jnp.where(high == k, take(source, low), value)
                value = jnp.where(used, value, 0.0)
                for out_ref in (left_ref, right_ref):
                    out_ref[b * 64 + r : b * 64 + r + 8, t * LANES : (t + 1) * LANES] = value
    product = product_ref[...].astype(jnp.float32)
    for out_ref, first, source in ((left_ref, 384, bits), (right_ref, 384, bits), (right_ref, 416, product)):
        out_ref[first : first + 32, :LANES] = source[:32]
        out_ref[first : first + 32, LANES:] = source[32:]


def split(value):
    high = value.astype(jnp.bfloat16)
    return high, (value - high.astype(jnp.float32)).astype(jnp.bfloat16)


def unpack_steps(packed_ref, bits, slots, put):
    per = LANES // slots
    present = bits > 0.5
    rank = (counts(bits) - bits).astype(jnp.int32)
    spare = per * slots < LANES
    index = jnp.where(present, rank, LANES - 1) if spare else jnp.minimum(rank, slots - 1)

    def one(q, k):
        def run():
            for t in range(BS // per):
                for b in range(BS):
                    parts = []
                    for r in (16 * q, 16 * q + 8):
                        where = index[r : r + 8] + slots * k
                        if spare:
                            where = jnp.minimum(where, LANES - 1)
                        source = packed_ref[b * 64 + r : b * 64 + r + 8, t * LANES : (t + 1) * LANES]
                        value = take(source, where)
                        if not spare:
                            value = jnp.where(present[r : r + 8], value, 0.0)
                        parts.append(value)
                    put(b, t * per + k, 16 * q, *split(jnp.concatenate(parts, axis=0)))

        return run

    return [one(q, k) for q in range(4) for k in range(per)]


def carried(packed_ref, first):
    rows = slice(first, first + 32)
    return jnp.concatenate([packed_ref[rows, :LANES], packed_ref[rows, LANES:]], axis=0)


def fetch(source_ref, target_ref):
    target_ref[...] = source_ref[...]


def left_kernel(count, where_ref, *refs):
    high_ref, low_ref, stack_ref = refs[-3:]
    step = pl.program_id(0)

    for k in range(count):
        pl.when(step == k)(functools.partial(fetch, refs[k], stack_ref))

    def put(b, c, r, high, low):
        rows = slice(b * 64 + r, b * 64 + r + 16)
        high_ref[0, rows, c * LANES : (c + 1) * LANES] = high
        low_ref[0, rows, c * LANES : (c + 1) * LANES] = low

    for run in unpack_steps(stack_ref, carried(stack_ref, 384), SLOTS_X, put):
        run()


def unpack_pair(stack_ref, bits, slots, core, high_ref, low_ref):
    steps = []
    for other in range(2):
        first = (core ^ other) * 64

        def put(b, c, r, high, low, first=first):
            rows = pl.ds(pl.multiple_of(first + (b * 128 + r), 16), 16)
            high_ref[rows, c * LANES : (c + 1) * LANES] = high
            low_ref[rows, c * LANES : (c + 1) * LANES] = low

        steps += unpack_steps(stack_ref.at[other], bits[other], slots, put)
    return steps


def multiply(left_high_ref, left_low_ref, high_ref, low_ref, total_ref, others):
    each = len(others) // 3
    for j in range(3):
        for run in others[each * j : each * (j + 1) if j < 2 else None]:
            run()
        span = slice(j * 256, (j + 1) * 256)
        part = dot(left_high_ref[0], high_ref[:, span]) + dot(left_high_ref[0], low_ref[:, span])
        total_ref[:, span] += part + dot(left_low_ref[0], high_ref[:, span])


def product(where_ref, blocks, bits_of, slots, lefts, work, begin, finish):
    stack_a, stack_b, high_a, low_a, high_b, low_b, total_ref = work
    step = pl.program_id(0)
    pairs = len(blocks) // 2
    last = pairs // 2 - 1
    core = where_ref[0] & 1

    def fetch_pair(pair, stack_ref):
        for other in range(2):
            fetch(blocks[pair + pairs * other], stack_ref.at[other])

    def unpack(pair, stack_ref, high_ref, low_ref):
        bits = [bits_of(2 * pair + other, stack_ref.at[other]) for other in range(2)]
        return unpack_pair(stack_ref, bits, slots, core, high_ref, low_ref)

    @pl.when(step == 0)
    def _():
        begin(total_ref)
        fetch_pair(0, stack_a)
        for run in unpack(0, stack_a, high_a, low_a):
            run()

    for k in range(last + 1):
        pl.when(step == k)(functools.partial(fetch_pair, 2 * k + 1, stack_b))

    multiply(*lefts[:2], high_a, low_a, total_ref, unpack(2 * step + 1, stack_b, high_b, low_b))

    for k in range(last):
        pl.when(step == k)(functools.partial(fetch_pair, 2 * k + 2, stack_a))

    @pl.when(step < last)
    def _():
        multiply(*lefts[2:], high_b, low_b, total_ref, unpack(2 * step + 2, stack_a, high_a, low_a))

    @pl.when(step == last)
    def _():
        multiply(*lefts[2:], high_b, low_b, total_ref, [])
        finish(total_ref)


def zero(total_ref):
    total_ref[...] = jnp.zeros_like(total_ref)


def square_kernel(where_ref, *refs):
    blocks, lefts = refs[:16], refs[16:20]
    pattern_ref, flag_x_ref = refs[20:22]
    out_ref, near_ref, away_ref = refs[22:25]

    def finish(total_ref):
        bits = pattern_ref[...].astype(jnp.float32)
        present = bits > 0.5
        position, group, most = slot_sources(bits, SLOTS_S)
        first_rows = where_ref[0] * 64 + lax.broadcasted_iota(jnp.int32, (64, LANES), 0)
        unit = jnp.where(first_rows == where_ref[1] * LANES + lanes_of(), 1.0, 0.0)
        position = jnp.minimum(position, LANES - 1)
        sums = jnp.zeros((8, LANES), jnp.float32)
        for r in range(0, 64, 8):
            here, kept, eye, second = position[r : r + 8], present[r : r + 8], unit[r : r + 8], group[r : r + 8] > 0
            for b in range(BS):
                rows = slice(b * 64 + r, b * 64 + r + 8)
                for t in range(3):
                    values = []
                    for c in (2 * t, 2 * t + 1):
                        square = total_ref[rows, c * LANES : (c + 1) * LANES]
                        gap = jnp.where(kept, square - eye if b == c else square, 0.0)
                        sums = sums + gap * gap
                        values.append(take(3.0 * eye - square if b == c else -square, here))
                    out_ref[rows, t * LANES : (t + 1) * LANES] = jnp.where(second, values[1], values[0])
        flag = jnp.maximum(flag_of(most, SLOTS_S), flag_x_ref[...])
        out_ref[384:392, :LANES] = jnp.full((8, LANES), jnp.sum(sums), jnp.float32)
        out_ref[384:392, LANES : 2 * LANES] = flag
        out_ref[384:392, 2 * LANES :] = flag
        for k, block_ref in enumerate(blocks):
            kept_ref = (near_ref, away_ref)[k // 4 % 2]
            kept_ref[2 * (k % 4) + k // 8] = carried(block_ref, 416)

    bits_of = lambda slot, packed_ref: carried(packed_ref, 384)
    product(where_ref, blocks, bits_of, SLOTS_X, lefts, refs[25:], zero, finish)


def first_next_kernel(where_ref, *refs):
    blocks, lefts = refs[:8], refs[8:12]
    patterns_ref, out_ref = refs[12:14]

    def finish(total_ref):
        out_ref[...] = total_ref[...]

    product(where_ref, blocks, lambda slot, packed_ref: patterns_ref[slot], SLOTS_S, lefts, refs[14:], zero, finish)


def next_kernel(where_ref, *refs):
    blocks, lefts = refs[:8], refs[8:12]
    patterns_ref, before_ref, pattern_ref = refs[12:15]
    out_ref, tall_ref = refs[15:17]

    def begin(total_ref):
        total_ref[...] = before_ref[...]

    def finish(total_ref):
        present = pattern_ref[...] > 0
        for b in range(BS):
            rows = slice(b * 64, (b + 1) * 64)
            for c in range(BS):
                span = slice(c * LANES, (c + 1) * LANES)
                total_ref[rows, span] = jnp.where(present, 0.5 * total_ref[rows, span], 0.0)
        for j in range(BS):
            lane = lanes_of() + j * LANES
            molecule = (lane * 10923) >> 16
            function = lane - molecule * BS
            for b in range(BS):
                value = jnp.zeros((64, LANES), jnp.float32)
                for c in range(BS):
                    source = total_ref[b * 64 : (b + 1) * 64, c * LANES : (c + 1) * LANES]
                    value = jnp.where(function == c, take(source, molecule), value)
                tall_ref[pl.ds(j * 384 + b, 64, stride=BS), :] = value
            out_ref[:, j * LANES : (j + 1) * LANES] = tall_ref[j * 384 : (j + 1) * 384, :]

    product(where_ref, blocks, lambda slot, packed_ref: patterns_ref[slot], SLOTS_S, lefts, refs[17:], begin, finish)


ANY = pl.BlockSpec(memory_space=pl.ANY)
HELD = pl.BlockSpec(memory_space=pltpu.VMEM)


def whole(shape):
    return pl.BlockSpec(shape, lambda i, where: (0,) * len(shape))


def params():
    return pltpu.CompilerParams(vmem_limit_bytes=VMEM)


def f32(*shape):
    return jax.ShapeDtypeStruct(shape, jnp.float32)


def cost(us):
    return pl.CostEstimate(flops=int(us * 1_000_000_000), bytes_accessed=int(us * 500_000), transcendentals=0)


def pack(x, operand, product):
    return pl.pallas_call(
        pack_kernel,
        out_shape=(f32(416, WIDE_X), f32(448, WIDE_X), f32(8, LANES)),
        scratch_shapes=[pltpu.VMEM((BS * 384, LANES), jnp.float32)],
        compiler_params=params(),
        name="pack",
    )(x, operand, product)


def left_parts(where, blocks, first, earlier=()):
    count = len(blocks)
    part = pl.BlockSpec((1, 384, 768), lambda i, where: (row_place(where, i + first), 0, 0))
    return pl.pallas_call(
        functools.partial(left_kernel, count),
        grid_spec=pltpu.PrefetchScalarGridSpec(
            num_scalar_prefetch=1,
            grid=(count,),
            in_specs=[HELD] * count + [ANY] * len(earlier),
            out_specs=[part, part],
            scratch_shapes=[pltpu.VMEM((416, WIDE_X), jnp.float32)],
        ),
        out_shape=[jax.ShapeDtypeStruct((8, 384, 768), jnp.bfloat16)] * 2,
        input_output_aliases={1 + count + k: k for k in range(len(earlier))},
        compiler_params=params(),
        cost_estimate=cost(1.25 * count),
        name="left_parts",
    )(where, *blocks, *earlier)


def product_call(kernel, name, where, blocks, second, high, low, rest, outs, stack, scratch=()):
    pairs = len(blocks) // 2
    even = pl.BlockSpec((1, 384, 768), lambda i, where: (column_pair(where, second + i // 2, i % 2), 0, 0))
    odd = pl.BlockSpec((1, 384, 768), lambda i, where: (column_pair(where, second + i // 2, 3 - i % 2), 0, 0))
    return pl.pallas_call(
        kernel,
        grid_spec=pltpu.PrefetchScalarGridSpec(
            num_scalar_prefetch=1,
            grid=(pairs // 2,),
            in_specs=[HELD] * len(blocks) + [even, even, odd, odd] + [whole(t.shape) for t in rest],
            out_specs=[whole(shape) for shape in outs],
            scratch_shapes=[*scratch]
            + [pltpu.VMEM((2, *stack), jnp.float32)] * 2
            + [pltpu.VMEM((768, 768), jnp.bfloat16)] * 4
            + [pltpu.VMEM((384, 768), jnp.float32)],
        ),
        out_shape=[f32(*shape) for shape in outs],
        compiler_params=params(),
        cost_estimate=cost(2.5 * pairs),
        name=name,
    )(where, *blocks, high, low, high, low, *rest)


def after(value, *earlier):
    return lax.optimization_barrier((value, *earlier))[0]


GATES = {"U": ("H",), "u": ("l",), "D": ("F",), "d": ("f",)}
GATES_S = {"C": ("U",), "CH": ("F",)}


def run_moves(table, gates, done):
    def get(name):
        if name not in done:
            source, move = table[name]
            value = get(source)
            if name in gates:
                value = after(value, *(get(g) for g in gates[name]))
            done[name] = send(value, move)
        return done[name]

    for name in table:
        get(name)
    return done


def both_blocks(left, right):
    table = dict([
        ("H", ("R", along(xh=1))),
        ("l", ("L", along(xl=1))),
        ("U", ("R", along(z=1))),
        ("u", ("L", along(y=1))),
        ("D", ("R", along(z=-1))),
        ("d", ("L", along(y=-1))),
        ("F", ("R", along(z=2))),
        ("f", ("L", along(y=2))),
        ("C", ("R", along(core=1))),
        ("HU", ("H", along(z=1))),
        ("lu", ("l", along(y=1))),
        ("HD", ("H", along(z=-1))),
        ("ld", ("l", along(y=-1))),
        ("HF", ("F", along(xh=1))),
        ("lf", ("f", along(xl=1))),
        ("CU", ("U", along(core=1))),
        ("CD", ("D", along(core=1))),
        ("CF", ("F", along(core=1))),
        ("CH", ("H", along(core=1))),
        ("CHU", ("HU", along(core=1))),
        ("CHD", ("HD", along(core=1))),
        ("CHF", ("HF", along(core=1))),
    ])
    done = run_moves(table, GATES, {"R": right, "L": left})
    near = [done[k] for k in ("R", "U", "D", "F", "C", "CU", "CD", "CF")]
    away = [done[k] for k in ("H", "HU", "HD", "HF", "CH", "CHU", "CHD", "CHF")]
    row = [done[k] for k in ("L", "u", "d", "f", "l", "lu", "ld", "lf")]
    return row, near, away


def column_blocks(own):
    table = dict([
        ("U", ("R", along(z=1))),
        ("D", ("R", along(z=-1))),
        ("H", ("R", along(xh=1))),
        ("F", ("R", along(z=2))),
        ("C", ("R", along(core=1))),
        ("HU", ("H", along(z=1))),
        ("HD", ("H", along(z=-1))),
        ("CU", ("U", along(core=1))),
        ("CD", ("D", along(core=1))),
        ("CH", ("H", along(core=1))),
        ("HF", ("F", along(xh=1))),
        ("CF", ("F", along(core=1))),
        ("CHU", ("HU", along(core=1))),
        ("CHD", ("HD", along(core=1))),
        ("CHF", ("HF", along(core=1))),
    ])
    done = run_moves(table, GATES_S, {"R": own})
    near = [done[k] for k in ("R", "U", "D", "F", "C", "CU", "CD", "CF")]
    away = [done[k] for k in ("H", "HU", "HD", "HF", "CH", "CHU", "CHD", "CHF")]
    return near, away


def column_pair(where, second, b):
    row = where[0]
    return ((row >> 3) ^ second) * 4 + (((row >> 1) + b) & 3)


def row_place(where_ref, k):
    col = where_ref[1]
    place = k & 3
    b = jnp.where(place == 0, 0, jnp.where(place == 1, 3, place - 1))
    return ((col >> 2) ^ (k >> 2)) * 4 + ((col + b) & 3)


def expand_blocks(pattern):
    rows, cols = pattern.shape
    wide = jnp.broadcast_to(pattern.astype(jnp.float32)[:, None, :, None], (rows, BS, cols, BS))
    return wide.reshape(rows * BS, cols * BS)


def matmul_high(left, right):
    return jnp.dot(left, right, precision=lax.Precision.HIGHEST, preferred_element_type=jnp.float32)


def gathered(value, name, axis):
    count = lax.axis_size(name)
    here = lax.axis_index(name)
    ring = [(i, (i + 1) % count) for i in range(count)]

    def body(k, state):
        value, kept = state
        kept = lax.dynamic_update_slice_in_dim(kept, value, (here - k + count) % count * value.shape[axis], axis)
        return lax.ppermute(value, name, ring), kept

    shape = [n * count if d == axis else n for d, n in enumerate(value.shape)]
    return lax.fori_loop(0, count, body, (value, jnp.zeros(shape, value.dtype)))[1]


def full_rows(sign_iterate, operand_pattern, product_pattern):
    local_rows, local_cols = sign_iterate.shape
    product_mask = expand_blocks(product_pattern)
    sparse_iterate = sign_iterate * expand_blocks(operand_pattern)
    entry_rows = lax.axis_index("row") * local_rows + jnp.arange(local_rows, dtype=jnp.int32)
    entry_cols = lax.axis_index("col") * local_cols + jnp.arange(local_cols, dtype=jnp.int32)
    identity = (entry_rows[:, None] == entry_cols[None, :]).astype(jnp.float32)
    left = gathered(sparse_iterate, "col", 1)
    square = matmul_high(left, gathered(sparse_iterate, "row", 0)) * product_mask
    polynomial = 3.0 * identity - square
    sign_next = 0.5 * matmul_high(left, gathered(polynomial, "row", 0)) * product_mask
    defect = jnp.sum((square - identity) ** 2).reshape(1, 1)
    for move in (along(core=1), along(xh=1), along(z=2), flip("z"), along(xl=1), along(y=2), flip("y")):
        defect = defect + send(defect, move)
    return sign_next, defect[0, 0]


def sum_of(blocks):
    own, up, down, far = (a[384:385, :256] + b[384:385, :256] for a, b in zip(blocks[:4], blocks[4:]))
    return (own + far) + (up + down)


def per_device(sign_iterate, operand_pattern, product_pattern):
    left, right, flag_x = pack(sign_iterate, operand_pattern, product_pattern)
    where = jnp.stack([lax.axis_index("row"), lax.axis_index("col")]).astype(jnp.int32)
    row, near, away = both_blocks(left, right)
    high, low = left_parts(where, row[:6], 0)
    high, low = left_parts(where, row[6:], 6, (high, low))
    total = (384, 768)
    eight = (8, 64, LANES)
    square, near_patterns, away_patterns = product_call(
        square_kernel, "square", where, near[:4] + away[:4] + near[4:] + away[4:], 0, high, low,
        (product_pattern, flag_x), ((392, WIDE_S), eight, eight), (448, WIDE_X),
    )

    near, away = column_blocks(square)
    (begun,) = product_call(
        first_next_kernel, "first_next", where, near, 0, high, low, (near_patterns,), (total,), (392, WIDE_S)
    )
    part = sum_of(near)
    for move in (along(y=2), flip("y"), along(xh=1), along(xl=1)):
        part = part + send(part, move)
    (sign_next,) = product_call(
        next_kernel, "next_iterate", where, away, 1, high, low, (away_patterns, begun, product_pattern),
        (total,), (392, WIDE_S), (pltpu.VMEM((BS * 384, LANES), jnp.float32),),
    )
    return lax.cond(
        part[0, LANES] > 0.0,
        lambda: full_rows(sign_iterate, operand_pattern, product_pattern),
        lambda: (sign_next, part[0, 0]),
    )


def flip(axis):
    if axis == "z":
        return lambda a, b, c, d, e: (a, b ^ 1, c, d, e)
    return lambda a, b, c, d, e: (a, b, c, d, e ^ 1)


def solution(mesh):
    spec = P("row", "col")
    return jax.shard_map(
        per_device, mesh=mesh, in_specs=(spec, spec, spec), out_specs=(spec, P()), check_vma=False
    )
```
